256 devices in a mesh: ctx: 32 (over x, y, core), grp: 8 (over z).
Axes of the slice: x: 4, y: 4, z: 8, core: 2. Of those that a mesh axis runs over, the one named last changes fastest.
Arguments:
- window_states: bfloat16 [8, 64, 8192], P('grp'), may hold values from -6 to 6
- query_weight: bfloat16 [8192, 8192], P('grp', 'ctx'), may hold values from -0.0625 to 0.0625
- cache_keys: bfloat16 [8, 16384, 1024], P('grp', 'ctx'), may hold values from -65 to 65
- cache_values: bfloat16 [8, 16384, 1024], P('grp', 'ctx'), may hold values from -6 to 6
- kept_blocks: int32 [8, 8, 32], P('grp', None, 'ctx'), may hold values from 0 to 127, as said below
- retained_block_count: int32 [8, 8, 32], P('grp', None, 'ctx'), may hold values from 0 to 1, as said below
- decode_queries: bfloat16 [8, 4, 32, 8192], P('grp', None, 'ctx'), may hold values from -9 to 9
- tail_keys: bfloat16 [8, 32, 64, 1024], P('grp', 'ctx'), may hold values from -6 to 6
- tail_values: bfloat16 [8, 32, 64, 1024], P('grp', 'ctx'), may hold values from -6 to 6
- row_lengths: int32 [8, 32], P('grp', 'ctx'), may hold values from 2 to 61, as said below
Outputs:
- pooled_votes: float32 [8, 8, 16384], P('grp', None, 'ctx')
- decode_out: bfloat16 [8, 4, 32, 8192], P('grp', None, 'ctx')
The draws below stay inside these ranges and needn't reach their ends.
Inputs may be any that keep to these rules, and one draw needn't show every extreme that they name: `kept_blocks`: for key head k, entry c names one block held by ctx index c, that is one of the blocks c * 4 to c * 4 + 3; it is kept only if retained_block_count[g, k, c] is 1. `retained_block_count`: in every request some device holds 1 kept blocks for every key head. `row_lengths`: 61 is reached in every request.
All inputs are finite; a program needn't handle non-finite values.
Results may differ from the reference program's by a relative error of at most 0.0019.
Values may be sent and summed in bfloat16 or wider, within the bound.
A program may use at most 128 MiB of HBM per device.

```python
import math
import jax
import jax.numpy as jnp
from jax import lax

D = 8192
H = 64
KEY_HEADS = 8
HEAD_DIMENSION = 128
CTX_DEV = 512
WIN = 64
BLOCK_POSITIONS = 128
POOL = 7
STEPS = 4
TAIL = 61
REQUEST_COUNT = 8
CTX = 16384
DROWS = 32
LBLK = 4
NBLK = 128
KEPT_LIMIT = 1
SLOT_COUNT = 32
TAILMAX = 64


def device_order(order_key):
    return jax.random.permutation(order_key, CTX // CTX_DEV)


def kept_plan(key):
    ctx_count = CTX // CTX_DEV
    hot_total = max(1, ctx_count // 8)
    orders = jax.vmap(device_order)(jax.random.split(jax.random.fold_in(key, 11), REQUEST_COUNT))
    hot_mask = jnp.any(orders[:, :hot_total, None] == jnp.arange(ctx_count)[None, None, :], axis=1)
    sparse = jnp.minimum(jax.random.randint(jax.random.fold_in(key, 12), (REQUEST_COUNT, KEY_HEADS, ctx_count), 0, 4), KEPT_LIMIT)
    counts = jnp.where(hot_mask[:, None, :], KEPT_LIMIT, sparse)
    ranking = jax.random.randint(jax.random.fold_in(key, 13), (REQUEST_COUNT, KEY_HEADS, ctx_count, LBLK), 0, 2 ** 20) * LBLK + jnp.arange(LBLK)
    picked = jnp.argsort(ranking, axis=-1)[..., :KEPT_LIMIT]
    blocks = picked + (jnp.arange(ctx_count) * LBLK)[None, None, :, None]
    return (blocks.reshape(REQUEST_COUNT, KEY_HEADS, ctx_count * KEPT_LIMIT).astype(jnp.int32), counts.astype(jnp.int32))


def draw_kept_blocks(key, part):
    return kept_plan(key)[0]


def draw_retained_block_count(key, part):
    return kept_plan(key)[1]


def draw_row_lengths(key, part):
    lengths = jax.random.randint(jax.random.fold_in(key, 21), (REQUEST_COUNT, DROWS), 2, TAIL + 1)
    longest = jax.random.randint(jax.random.fold_in(key, 22), (REQUEST_COUNT, 1), 0, DROWS)
    return jnp.where(jnp.arange(DROWS)[None, :] == longest, TAIL, lengths).astype(jnp.int32)


def draw_cache_keys(key, part):
    shape_all = (REQUEST_COUNT, CTX, KEY_HEADS * HEAD_DIMENSION)
    growth = 1.0 + 0.8 * jnp.arange(CTX).astype(jnp.float32) / CTX
    base_draw = jnp.clip(jax.random.normal(key, shape_all, jnp.float32), -6.0, 6.0)
    base_draw = base_draw * growth[None, :, None]
    return base_draw.astype(jnp.bfloat16)


def draw_decode_queries(key, part):
    shape_all = (REQUEST_COUNT, STEPS, DROWS, H * HEAD_DIMENSION)
    base_draw = jnp.clip(jax.random.normal(key, shape_all, jnp.float32), -6.0, 6.0)
    return base_draw.astype(jnp.bfloat16)


def draw_tail_keys(key, part):
    shape_all = (REQUEST_COUNT, DROWS, TAILMAX, KEY_HEADS * HEAD_DIMENSION)
    base_draw = jnp.clip(jax.random.normal(key, shape_all, jnp.float32), -6.0, 6.0)
    return base_draw.astype(jnp.bfloat16)


def block_scale(key, dims, cuts, smallest, high):
    def one(dim, parts):
        heights = jax.random.uniform(jax.random.fold_in(jax.random.fold_in(key, 6), dim), (parts,), jnp.float32, smallest / len(cuts), high / len(cuts))
        return jnp.repeat(jnp.exp(heights), dims[dim] // parts).reshape((-1,) + (1,) * (len(dims) - dim - 1))

    factor_of = one(*cuts[0])
    for cut in cuts[1:]:
        factor_of = factor_of * one(*cut)
    return factor_of


def noise(own_key, shape, spread, reach, cuts=(), dtype=jnp.bfloat16):
    factor_of = block_scale(own_key, shape, cuts, -0.22, 0.18) if cuts else 1.0
    result = jax.random.normal(own_key, shape, jnp.float32) * spread * factor_of
    return jnp.minimum(jnp.maximum(result, -reach), reach).astype(dtype)


def setup_inputs(seed: int = 0) -> dict:
    key_list = jax.random.split(jax.random.key(seed), 11)
    return {
        "window_states": noise(key_list[0], (REQUEST_COUNT, WIN, D), 1.0, 6.0, ((0, 8),)),
        "query_weight": noise(key_list[1], (D, H * HEAD_DIMENSION), D ** -0.5, 0.0625, ((0, 8), (1, 32))),
        "cache_keys": draw_cache_keys(jax.random.fold_in(key_list[10], 71), 0),
        "cache_values": noise(key_list[3], (REQUEST_COUNT, CTX, KEY_HEADS * HEAD_DIMENSION), 1.0, 6.0, ((0, 8), (1, 32))),
        "kept_blocks": draw_kept_blocks(jax.random.fold_in(key_list[10], 71), 0),
        "retained_block_count": draw_retained_block_count(jax.random.fold_in(key_list[10], 71), 0),
        "decode_queries": draw_decode_queries(jax.random.fold_in(key_list[10], 71), 0),
        "tail_keys": draw_tail_keys(jax.random.fold_in(key_list[10], 71), 0),
        "tail_values": noise(key_list[8], (REQUEST_COUNT, DROWS, TAILMAX, KEY_HEADS * HEAD_DIMENSION), 1.0, 6.0, ((0, 8), (1, 32))),
        "row_lengths": draw_row_lengths(jax.random.fold_in(key_list[10], 71), 0),
    }


def rotary_table(positions, head_size):
    exponent = jnp.arange(0, head_size, 2).astype(jnp.float32) / head_size
    inverse = jnp.power(jnp.float32(500000.0), -exponent)
    wavelength = 2.0 * math.pi / inverse
    smooth = (8192.0 / wavelength - 1.0) / 3.0
    blended = (1.0 - smooth) * inverse / 8.0 + smooth * inverse
    adjusted = jnp.where(wavelength > 8192.0, inverse / 8.0, jnp.where(wavelength < 2048.0, inverse, blended))
    angles = positions[:, None] * adjusted[None, :]
    return (jnp.cos(angles), jnp.sin(angles))

def rotate(vectors, cosine_table, sine_table):
    half_size = vectors.shape[-1] // 2
    leading = vectors[..., :half_size]
    trailing = vectors[..., half_size:]
    cosine_part = cosine_table[:, None, :]
    sine_part = sine_table[:, None, :]
    return jnp.concatenate([leading * cosine_part - trailing * sine_part, trailing * cosine_part + leading * sine_part], axis=-1)

def reference(window_states, query_weight, cache_keys, cache_values, kept_blocks, retained_block_count, decode_queries, tail_keys, tail_values, row_lengths):
    group_size = H // KEY_HEADS
    key_scale = 1.0 / math.sqrt(HEAD_DIMENSION)
    start_pos = CTX - WIN
    positions = (jnp.arange(WIN) + start_pos).astype(jnp.float32)
    cosine_table, sine_table = rotary_table(positions, HEAD_DIMENSION)

    def window_rows(states):
        projected = jnp.dot(states, query_weight, preferred_element_type=jnp.float32)
        turned = rotate(projected.reshape(WIN, H, HEAD_DIMENSION), cosine_table, sine_table)
        return turned.reshape(WIN, H * HEAD_DIMENSION).astype(jnp.bfloat16)
    window_queries = lax.map(window_rows, window_states)
    allowed = jnp.arange(CTX)[None, :] <= (jnp.arange(WIN) + start_pos)[:, None]

    def vote_head(inputs):
        head_queries, key_head_rows = inputs
        scores = jnp.einsum('wgd,td->gwt', head_queries.astype(jnp.float32), key_head_rows.astype(jnp.float32)) * key_scale
        scores = jnp.where(allowed[None], scores, -1e+30)
        peak_value = lax.optimization_barrier(jnp.max(scores, axis=-1, keepdims=True))
        weights = jnp.where(allowed[None], jnp.exp(scores - peak_value), 0.0)
        probability = weights / lax.optimization_barrier(jnp.sum(weights, axis=-1, keepdims=True))
        return lax.optimization_barrier(jnp.sum(probability, axis=(0, 1))) * (CTX / (WIN * group_size))

    def vote_group(inputs):
        group_queries, group_keys = inputs
        per_query = group_queries.reshape(WIN, KEY_HEADS, group_size, HEAD_DIMENSION).transpose(1, 0, 2, 3)
        per_key = group_keys.reshape(CTX, KEY_HEADS, HEAD_DIMENSION).transpose(1, 0, 2)
        return lax.map(vote_head, (per_query, per_key))
    vote_sums = lax.map(vote_group, (window_queries, cache_keys))
    half_width = (POOL - 1) // 2
    padded = jnp.pad(vote_sums, ((0, 0), (0, 0), (half_width, half_width)))
    pooled = padded[:, :, 0:CTX]
    for shift_index in range(1, POOL):
        pooled = pooled + padded[:, :, shift_index:shift_index + CTX]
    pooled_votes = pooled / POOL
    slot_active_mask = (jnp.arange(KEPT_LIMIT)[None, None, None, :] < retained_block_count[:, :, :, None]).reshape(REQUEST_COUNT, KEY_HEADS, SLOT_COUNT)
    steps_range = jnp.arange(STEPS)

    def decode_group(inputs):
        group_queries, group_keys, group_values, group_blocks, group_live, group_tkeys, group_tvalues, group_lengths = inputs
        visible = jnp.arange(TAILMAX)[None, None, :] < group_lengths[None, :, None] + steps_range[:, None, None]
        per_query = group_queries.reshape(STEPS, DROWS, KEY_HEADS, group_size, HEAD_DIMENSION).transpose(2, 0, 1, 3, 4)
        per_key = group_keys.reshape(NBLK, BLOCK_POSITIONS, KEY_HEADS, HEAD_DIMENSION).transpose(2, 0, 1, 3)
        per_value = group_values.reshape(NBLK, BLOCK_POSITIONS, KEY_HEADS, HEAD_DIMENSION).transpose(2, 0, 1, 3)
        tail_key_heads = group_tkeys.reshape(DROWS, TAILMAX, KEY_HEADS, HEAD_DIMENSION).transpose(2, 0, 1, 3)
        tail_value_heads = group_tvalues.reshape(DROWS, TAILMAX, KEY_HEADS, HEAD_DIMENSION).transpose(2, 0, 1, 3)

        def decode_head(head_inputs):
            head_queries, key_head_rows, value_head_rows, per_head_blocks, head_active_mask, head_tkeys, head_tvalues = head_inputs
            selected_keys = key_head_rows[per_head_blocks.astype(jnp.int32)].reshape(SLOT_COUNT * BLOCK_POSITIONS, HEAD_DIMENSION).astype(jnp.float32)
            selected_values = value_head_rows[per_head_blocks.astype(jnp.int32)].reshape(SLOT_COUNT * BLOCK_POSITIONS, HEAD_DIMENSION).astype(jnp.float32)
            key_active_mask = jnp.repeat(head_active_mask, BLOCK_POSITIONS, total_repeat_length=SLOT_COUNT * BLOCK_POSITIONS)
            query_float = head_queries.astype(jnp.float32)
            cache_scores = jnp.einsum('srgd,td->srgt', query_float, selected_keys) * key_scale
            cache_scores = jnp.where(key_active_mask, cache_scores, -1e+30)
            tail_scores = jnp.einsum('srgd,rjd->srgj', query_float, head_tkeys.astype(jnp.float32)) * key_scale
            tail_scores = jnp.where(visible[:, :, None, :], tail_scores, -1e+30)
            peak_value = jnp.maximum(lax.optimization_barrier(jnp.max(cache_scores, axis=-1)), lax.optimization_barrier(jnp.max(tail_scores, axis=-1)))[..., None]
            cache_weights = jnp.where(key_active_mask, jnp.exp(cache_scores - peak_value), 0.0)
            tail_weights = jnp.where(visible[:, :, None, :], jnp.exp(tail_scores - peak_value), 0.0)
            numerator = jnp.einsum('srgt,td->srgd', cache_weights, selected_values, precision=lax.Precision.HIGHEST)
            numerator = numerator + jnp.einsum('srgj,rjd->srgd', tail_weights, head_tvalues.astype(jnp.float32), precision=lax.Precision.HIGHEST)
            denominator = lax.optimization_barrier(jnp.sum(cache_weights, axis=-1)) + lax.optimization_barrier(jnp.sum(tail_weights, axis=-1))
            return numerator / denominator[..., None]
        per_head = lax.map(decode_head, (per_query, per_key, per_value, group_blocks, group_live, tail_key_heads, tail_value_heads))
        return per_head.transpose(1, 2, 0, 3, 4).reshape(STEPS, DROWS, H * HEAD_DIMENSION).astype(jnp.bfloat16)
    decode_out = lax.map(decode_group, (decode_queries, cache_keys, cache_values, kept_blocks, slot_active_mask, tail_keys, tail_values, row_lengths))
    return (pooled_votes, decode_out)
```

```python
import math

import jax
import jax.numpy as jnp
import numpy as np
from jax import lax
from jax.experimental import pallas as pl
from jax.experimental.pallas import tpu as pltpu
from jax.sharding import PartitionSpec as P

MESH = pl.DeviceIdType.MESH
F32 = jnp.float32
BF16 = jnp.bfloat16
KEY_HEADS = 8
HEAD_DIMENSION = 128
BLOCK = 128
POOL = 7
WIN = 64
STEPS = 4
CHIPS = 16
GROUPS = 8
POSITIONS = 512
SPAN = 2 * POSITIONS
EDGE = 16
ROWS = SPAN + 2 * EDGE
PIECE = 96
NPIECE = ROWS // PIECE
KV_ROWS = 2 * BLOCK + 16
QT_ROWS = 192
LOW = -1e30
SCALE = 1.0 / math.sqrt(HEAD_DIMENSION)
NT = (((1,), (1,)), ((), ()))


def rotary_table():
    exponent = np.arange(0, HEAD_DIMENSION, 2).astype(np.float32) / np.float32(HEAD_DIMENSION)
    inverse = np.power(np.float32(500000.0), -exponent).astype(np.float32)
    wavelength = np.float32(2.0 * math.pi) / inverse
    smooth = (np.float32(8192.0) / wavelength - np.float32(1.0)) / np.float32(3.0)
    blended = (np.float32(1.0) - smooth) * inverse / np.float32(8.0) + smooth * inverse
    adjusted = np.where(
        wavelength > 8192.0,
        inverse / np.float32(8.0),
        np.where(wavelength < 2048.0, inverse, blended),
    ).astype(np.float32)
    start = 2 * CHIPS * POSITIONS - WIN
    positions = (np.arange(WIN) + start).astype(np.float32)
    angles = (positions[:, None] * adjusted[None, :]).astype(np.float32).astype(np.float64)
    cosine, sine = np.cos(angles), np.sin(angles)
    return (
        np.concatenate([cosine, cosine], axis=1).astype(np.float32),
        np.concatenate([-sine, sine], axis=1).astype(np.float32),
    )


def dot(a, b):
    return jnp.dot(a, b, preferred_element_type=F32)


def dot_nt(a, b):
    return lax.dot_general(a, b, NT, preferred_element_type=F32)


def body(
    states,
    weight,
    keys,
    values,
    kept,
    counts,
    queries,
    tail_keys,
    tail_values,
    lengths,
    cosine,
    sine,
    votes_out,
    decode_out,
    w_both,
    keys_own,
    values_own,
    keys_span,
    gathered,
    partial,
    parts,
    window,
    exps,
    stat,
    stat_in,
    total,
    total_in,
    columns,
    pooled,
    pooled_in,
    kv_out,
    kv_in,
    qt_out,
    qt_in,
    dec_scores,
    tail_scores,
    dec_send,
    dec_in,
    local_sem,
    piece_send,
    piece_recv,
    gather_send,
    gather_recv,
    pair_send,
    pair_recv,
    part_send,
    part_recv,
    window_send,
    window_recv,
    stat_send,
    stat_recv,
    total_send,
    total_recv,
    kv_send,
    kv_recv,
    fwd_send,
    fwd_recv,
    qt_send,
    qt_recv,
    dec_send_sem,
    dec_recv,
):
    c = lax.axis_index("ctx")
    z = lax.axis_index("grp")
    p = c // 2
    j = c % 2
    sibling = 2 * p + (1 - j)
    half = p // 8
    slot = p % 8

    def remote(src, dst, send_sem, recv_sem, ctx, grp):
        return pltpu.make_async_remote_copy(
            src_ref=src,
            dst_ref=dst,
            send_sem=send_sem,
            recv_sem=recv_sem,
            device_id=(ctx, grp),
            device_id_type=MESH,
        )

    def core_of(chip):
        return 2 * chip + j

    def each(low, high, step):
        def go(i, carry):
            step(i)
            return carry

        lax.fori_loop(low, high, go, 0)

    own_rows = pl.ds(pl.multiple_of(EDGE + j * POSITIONS, 16), POSITIONS)
    load_w = pltpu.make_async_copy(weight, w_both.at[j], local_sem.at[0])
    load_k = pltpu.make_async_copy(keys.at[0], keys_own, local_sem.at[1])
    load_v = pltpu.make_async_copy(values.at[0], values_own, local_sem.at[2])
    load_span = pltpu.make_async_copy(keys.at[0], keys_span.at[own_rows], local_sem.at[3])
    row0 = pl.multiple_of(32 * j + 16 * (p // 8), 16)

    def piece_of(g):
        col0 = pl.multiple_of(g * 1024 + 128 * (p % 8), 128)
        return states.at[0, pl.ds(row0, 16), pl.ds(col0, 128)]

    load_piece = pltpu.make_async_copy(piece_of(z), gathered.at[p, z], local_sem.at[4])

    def qt_load(k):
        cols = pl.ds(pl.multiple_of(k * 128, 128), 128)
        return (
            pltpu.make_async_copy(
                tail_keys.at[0, 0, :, cols], qt_out.at[k, pl.ds(0, 64)], local_sem.at[8 + k]
            ),
            pltpu.make_async_copy(
                tail_values.at[0, 0, :, cols], qt_out.at[k, pl.ds(64, 64)], local_sem.at[16 + k]
            ),
            pltpu.make_async_copy(
                queries.at[k], qt_out.at[k, pl.ds(128, 32)], local_sem.at[24 + k]
            ),
        )

    load_piece.start()
    load_k.start()
    load_v.start()
    load_w.start()
    load_span.start()

    def qt_start(k):
        for copy in qt_load(k):
            copy.start()

    each(0, KEY_HEADS, qt_start)

    barrier = pltpu.get_barrier_semaphore()

    def greet(ctx, grp):
        pl.semaphore_signal(barrier, inc=1, device_id=(ctx, grp), device_id_type=MESH)

    each(1, CHIPS, lambda d: greet(core_of(lax.rem(p + d, CHIPS)), z))
    greet(sibling, z)

    def greet_group(d):
        g = lax.rem(z + d, GROUPS)
        greet(c, g)
        greet(sibling, g)

    each(1, GROUPS, greet_group)
    pl.semaphore_wait(barrier, CHIPS - 1 + 1 + 2 * (GROUPS - 1))

    def piece_copy(g_to, slot_of):
        return remote(
            piece_of(g_to),
            gathered.at[p, slot_of],
            piece_send.at[g_to],
            piece_recv.at[slot_of],
            c,
            g_to,
        )

    each(1, GROUPS, lambda d: piece_copy(lax.rem(z + d, GROUPS), z).start())

    share_w = remote(weight, w_both.at[j], pair_send.at[0], pair_recv.at[0], sibling, z)
    share_k = remote(keys.at[0], keys_span.at[own_rows], pair_send.at[1], pair_recv.at[1], sibling, z)
    share_w.start()
    share_k.start()

    load_piece.wait()
    each(
        1,
        GROUPS,
        lambda d: piece_copy(
            lax.rem(z + GROUPS - d, GROUPS), lax.rem(z + GROUPS - d, GROUPS)
        ).wait_recv(),
    )

    def gather_copy(chip, source):
        return remote(
            gathered.at[source],
            gathered.at[source],
            gather_send.at[chip],
            gather_recv.at[source],
            core_of(chip),
            z,
        )

    each(1, CHIPS, lambda d: gather_copy(lax.rem(p + d, CHIPS), p).start())

    load_k.wait()
    load_v.wait()

    def kv_copy(k, side):
        chip = k + 8 * side
        return remote(
            kv_out.at[k],
            kv_in.at[j * CHIPS + p],
            kv_send.at[chip],
            kv_recv.at[p],
            core_of(chip),
            z,
        )

    kv_self = pltpu.make_async_copy(kv_out.at[slot], kv_in.at[j * CHIPS + p], local_sem.at[5])
    for k in range(KEY_HEADS):
        cols = slice(k * 128, (k + 1) * 128)
        block = kept[0, k, 0] - c * (POSITIONS // BLOCK)
        chosen = [
            jnp.where(jnp.full((BLOCK, 128), block, jnp.int32) == b, 1.0, 0.0).astype(BF16)
            for b in range(POSITIONS // BLOCK)
        ]
        for n, own in ((0, keys_own), (1, values_own)):
            kv_out[k, n * BLOCK : (n + 1) * BLOCK, :] = sum(
                chosen[b] * own[b * BLOCK : (b + 1) * BLOCK, cols]
                for b in range(POSITIONS // BLOCK)
            )
        live = jnp.full((16, 128), counts[0, k, 0], jnp.int32) > 0
        kv_out[k, 2 * BLOCK : KV_ROWS, :] = jnp.where(live, 0.0, LOW).astype(BF16)
        for side in range(2):

            @pl.when(k + 8 * side != p)
            def _():
                kv_copy(k, side).start()

    kv_self.start()

    step_row = lax.broadcasted_iota(jnp.int32, (32, 128), 0) // 8
    lane = lax.broadcasted_iota(jnp.int32, (32, 128), 1)
    tail_bias = jnp.where(lane < lengths[0, 0] + step_row, 0.0, LOW).astype(BF16)

    def qt_copy(k):
        return remote(
            qt_out.at[k],
            qt_in.at[slot],
            qt_send.at[k],
            qt_recv.at[slot],
            core_of(8 * half + k),
            z,
        )

    def qt_go(k):
        for copy in qt_load(k):
            copy.wait()
        qt_out[k, 160:QT_ROWS, :] = tail_bias

        @pl.when(k != slot)
        def _():
            qt_copy(k).start()

    each(0, KEY_HEADS, qt_go)
    qt_self = pltpu.make_async_copy(qt_out.at[slot], qt_in.at[slot], local_sem.at[6])
    qt_self.start()

    load_w.wait()
    share_w.wait_recv()
    each(
        1,
        CHIPS,
        lambda d: gather_copy(
            lax.rem(p + CHIPS - d, CHIPS), lax.rem(p + CHIPS - d, CHIPS)
        ).wait_recv(),
    )
    for core in range(2):
        for i in range(2):
            acc = jnp.zeros((128, 256), F32)
            for m in range(4):
                left = gathered[8 * i + 2 * m].reshape(128, 128)
                right = gathered[8 * i + 2 * m + 1].reshape(128, 128)
                acc = acc + dot(
                    jnp.concatenate([left, right], axis=1),
                    w_both[core, 256 * m : 256 * (m + 1), :],
                )
            partial[core, :, 16 * i : 16 * (i + 1), :] = acc.reshape(GROUPS, 16, 256)

    def part_copy(core, g_to, g_from, j_from):
        return remote(
            partial.at[core, g_to],
            parts.at[g_from, j_from],
            part_send.at[core, g_to],
            part_recv.at[g_from, j_from],
            2 * p + core,
            g_to,
        )

    def part_go(d):
        g = lax.rem(z + d, GROUPS)
        part_copy(0, g, z, j).start()
        part_copy(1, g, z, j).start()

    each(1, GROUPS, part_go)
    part_copy(1 - j, z, z, j).start()
    parts[z, j] = partial[j, z]

    load_span.wait()
    share_k.wait_recv()

    def edge_copy(up):
        src = keys_span.at[pl.ds(SPAN if up else EDGE, EDGE)]
        dst = keys_span.at[pl.ds(0 if up else SPAN + EDGE, EDGE)]
        chip = p + 1 if up else p - 1
        n = 2 + int(up)
        return remote(src, dst, pair_send.at[n], pair_recv.at[n], core_of(chip), z)

    @pl.when(p < CHIPS - 1)
    def _():
        edge_copy(True).start()

    @pl.when(p > 0)
    def _():
        edge_copy(False).start()

    @pl.when(p == 0)
    def _():
        keys_span[0:EDGE, :] = jnp.zeros((EDGE, 1024), BF16)

    @pl.when(p == CHIPS - 1)
    def _():
        keys_span[SPAN + EDGE : ROWS, :] = jnp.zeros((EDGE, 1024), BF16)

    kv_self.wait()

    def kv_wait(source):
        @pl.when(source != p)
        def _():
            remote(
                kv_in.at[j * CHIPS + source],
                kv_in.at[j * CHIPS + source],
                kv_send.at[0],
                kv_recv.at[source],
                core_of(source),
                z,
            ).wait_recv()

    def fwd_copy(n, core):
        part = kv_in.at[pl.ds(core * CHIPS + 4 * n, 4)]
        return remote(part, part, fwd_send.at[n], fwd_recv.at[n], sibling, z)

    def fwd_go(n):
        each(4 * n, 4 * n + 4, kv_wait)
        fwd_copy(n, j).start()

    each(0, 4, fwd_go)

    def part_wait(d):
        g = lax.rem(z + GROUPS - d, GROUPS)
        part_copy(0, g, g, 0).wait_recv()
        part_copy(0, g, g, 1).wait_recv()

    each(1, GROUPS, part_wait)
    part_copy(0, z, z, 1 - j).wait_recv()
    for i in range(2):
        summed = parts[0, i]
        for g in range(1, GROUPS):
            summed = summed + parts[g, i]
        turn_c = cosine[32 * i : 32 * (i + 1), :]
        turn_s = sine[32 * i : 32 * (i + 1), :]
        for h in range(2):
            head = summed[:, 128 * h : 128 * (h + 1)]
            turned = head * turn_c + pltpu.roll(head, 64, axis=1) * turn_s
            window[p, h, 32 * i : 32 * (i + 1), :] = turned.astype(BF16)

    def window_copy(chip, source):
        return remote(
            window.at[source],
            window.at[source],
            window_send.at[chip],
            window_recv.at[source],
            core_of(chip),
            z,
        )

    each(1, CHIPS, lambda d: window_copy(lax.rem(p + d, CHIPS), p).start())

    qt_self.wait()

    def qt_wait(r):
        @pl.when(r != slot)
        def _():
            remote(
                qt_in.at[r], qt_in.at[r], qt_send.at[0], qt_recv.at[r], core_of(8 * half + r), z
            ).wait_recv()

    each(0, 8, qt_wait)
    each(0, 4, lambda n: fwd_copy(n, 1 - j).wait_recv())
    rows_q = qt_in[:, 128:160, :].reshape(256, 128)

    def tail_go(r):
        s = dot_nt(qt_in[r, 128:160, :], qt_in[r, 0:128, :]) * SCALE
        tail_scores[r] = s + qt_in[r, 160:QT_ROWS, :].astype(F32)

    each(0, 8, tail_go)
    top = tail_scores[...].reshape(256, 128)

    def score_go(b, top):
        s = dot_nt(rows_q, kv_in[b, 0:BLOCK, :]) * SCALE
        s = s + kv_in[b, 2 * BLOCK : KV_ROWS, :].astype(F32)[0:1, :]
        dec_scores[b] = s
        return jnp.maximum(top, s)

    top = lax.fori_loop(0, 2 * CHIPS, score_go, top)
    top = jnp.max(top, axis=1, keepdims=True)

    def split(weights):
        high = weights.astype(BF16)
        return high, (weights - high.astype(F32)).astype(BF16)

    tail_weights = jnp.exp(tail_scores[...].reshape(256, 128) - top)
    tail_acc = []
    for r in range(8):
        high, low = split(tail_weights[32 * r : 32 * (r + 1), :])
        right = qt_in[r, 64:QT_ROWS, :]
        tail_acc.append(dot(high, right) + dot(low, right))

    def value_go(b, carry):
        acc, weight_sum = carry
        weights = jnp.exp(dec_scores[b] - top)
        high, low = split(weights)
        right = kv_in[b, BLOCK : 2 * BLOCK, :]
        both = dot(jnp.concatenate([high, low], axis=1), jnp.concatenate([right, right], axis=0))
        return acc + both, weight_sum + weights

    acc, weight_sum = lax.fori_loop(
        0, 2 * CHIPS, value_go, (jnp.concatenate(tail_acc, axis=0), tail_weights)
    )
    result = acc / jnp.sum(weight_sum, axis=1, keepdims=True)
    dec_send[...] = result.astype(BF16).reshape(8, 32, 128)

    def dec_copy(r):
        return remote(
            dec_send.at[r],
            dec_in.at[slot],
            dec_send_sem.at[r],
            dec_recv.at[slot],
            core_of(8 * half + r),
            z,
        )

    def dec_go(r):
        @pl.when(r != slot)
        def _():
            dec_copy(r).start()

    each(0, 8, dec_go)
    dec_self = pltpu.make_async_copy(dec_send.at[slot], dec_in.at[slot], local_sem.at[7])
    dec_self.start()

    @pl.when(p > 0)
    def _():
        edge_copy(True).wait_recv()

    @pl.when(p < CHIPS - 1)
    def _():
        edge_copy(False).wait_recv()

    piece_row = lax.broadcasted_iota(jnp.int32, (PIECE, 256), 0)
    piece_lane = lax.broadcasted_iota(jnp.int32, (PIECE, 256), 1)
    hidden_first = jnp.logical_and(piece_row < EDGE, p == 0)
    last_row = piece_row + (NPIECE - 1) * PIECE
    hidden_last = jnp.logical_or(
        jnp.logical_and(last_row >= SPAN + EDGE, p == CHIPS - 1),
        jnp.logical_and(
            last_row < SPAN + EDGE,
            p * SPAN + last_row - EDGE
            > (2 * CHIPS * POSITIONS - WIN) + jnp.bitwise_and(piece_lane, WIN - 1),
        ),
    )

    def stat_copy(o):
        return remote(
            stat.at[o], stat_in.at[p], stat_send.at[o], stat_recv.at[p], core_of(o), z
        )

    def window_go(k):
        for n in range(2):
            source = 2 * k + n

            @pl.when(source != p)
            def _():
                window_copy(0, source).wait_recv()

        rows = window[pl.ds(2 * k, 2)].reshape(256, 128)
        cols = pl.ds(pl.multiple_of(k * 128, 128), 128)
        top = jnp.full((8, 256), LOW, F32)
        for i in range(NPIECE):
            s = dot_nt(keys_span[PIECE * i : PIECE * (i + 1), cols], rows) * SCALE
            if i == 0:
                s = jnp.where(hidden_first, LOW, s)
            if i == NPIECE - 1:
                s = jnp.where(hidden_last, LOW, s)
            exps[k, PIECE * i : PIECE * (i + 1), :] = s
            top = jnp.maximum(top, jnp.max(s.reshape(PIECE // 8, 8, 256), axis=0))
        top = jnp.max(top, axis=0, keepdims=True)
        summed = jnp.zeros((8, 256), F32)
        for i in range(NPIECE):
            e = jnp.exp(exps[k, PIECE * i : PIECE * (i + 1), :] - top)
            exps[k, PIECE * i : PIECE * (i + 1), :] = e
            if i == 0:
                e = e[EDGE:]
            if i == NPIECE - 1:
                e = e[: PIECE - EDGE]
            summed = summed + jnp.sum(e.reshape(-1, 8, 256), axis=0)
        summed = jnp.sum(summed, axis=0, keepdims=True)
        for n in range(2):
            o = 2 * k + n
            stat[o, 0:1, :] = top[:, 128 * n : 128 * (n + 1)]
            stat[o, 1:2, :] = summed[:, 128 * n : 128 * (n + 1)]

            @pl.when(o != p)
            def _():
                stat_copy(o).start()

    each(0, KEY_HEADS, window_go)
    stat_in[p] = stat[p]

    def stat_wait(d):
        source = lax.rem(p + CHIPS - d, CHIPS)
        remote(
            stat.at[source], stat_in.at[source], stat_send.at[0], stat_recv.at[source], core_of(source), z
        ).wait_recv()

    each(1, CHIPS, stat_wait)
    peak = stat_in[0, 0:1, :]
    for o in range(1, CHIPS):
        peak = jnp.maximum(peak, stat_in[o, 0:1, :])
    merged = jnp.zeros((1, 128), F32)
    for o in range(CHIPS):
        merged = merged + stat_in[o, 1:2, :] * jnp.exp(stat_in[o, 0:1, :] - peak)
    total[0:1, :] = peak
    total[1:2, :] = merged

    def total_copy(chip, source):
        return remote(
            total, total_in.at[source], total_send.at[chip], total_recv.at[source], core_of(chip), z
        )

    each(1, CHIPS, lambda d: total_copy(lax.rem(p + d, CHIPS), p).start())
    total_in[p] = total[...]

    dec_self.wait()

    def dec_wait(k):
        @pl.when(k != slot)
        def _():
            remote(
                dec_send.at[k], dec_in.at[k], dec_send_sem.at[0], dec_recv.at[k], core_of(8 * half + k), z
            ).wait_recv()

    each(0, 8, dec_wait)
    decode_out[...] = dec_in[...]

    each(
        1,
        CHIPS,
        lambda d: total_copy(
            lax.rem(p + CHIPS - d, CHIPS), lax.rem(p + CHIPS - d, CHIPS)
        ).wait_recv(),
    )

    factors = []
    for o in range(CHIPS):
        factors.append(
            jnp.exp(stat[o, 0:1, :] - total_in[o, 0:1, :]) / total_in[o, 1:2, :]
        )
    head_lane = lax.broadcasted_iota(jnp.int32, (PIECE, 128), 1)
    for i in range(NPIECE):
        rows = slice(PIECE * i, PIECE * (i + 1))
        votes = jnp.zeros((PIECE, 128), F32)
        for k in range(KEY_HEADS):
            weighted = (
                exps[k, rows, 0:128] * factors[2 * k] + exps[k, rows, 128:256] * factors[2 * k + 1]
            )
            votes = jnp.where(head_lane == k, jnp.sum(weighted, axis=1, keepdims=True), votes)
        columns[rows, :] = votes
    columns[ROWS:, :] = jnp.zeros((columns.shape[0] - ROWS, 128), F32)
    lanes = columns.shape[0]
    across = jnp.transpose(columns[...])[0:KEY_HEADS, :]
    near = POOL // 2
    window_sum = jnp.zeros((KEY_HEADS, lanes), F32)
    for shift in range(EDGE - near, EDGE + near + 1):
        window_sum = window_sum + pltpu.roll(across, lanes - shift, axis=1)
    for n in range(2):
        pooled[n] = window_sum[:, POSITIONS * n : POSITIONS * (n + 1)]
    share_votes = remote(pooled.at[1 - j], pooled_in, pair_send.at[4], pair_recv.at[4], sibling, z)
    share_votes.start()
    share_votes.wait_recv()
    votes_out[...] = (pooled[j] + pooled_in[...]) * (
        2 * CHIPS * POSITIONS / (WIN * 8) / POOL
    )

    share_votes.wait_send()
    share_w.wait_send()
    share_k.wait_send()

    @pl.when(p < CHIPS - 1)
    def _():
        edge_copy(True).wait_send()

    @pl.when(p > 0)
    def _():
        edge_copy(False).wait_send()

    def sent_group(d):
        g = lax.rem(z + d, GROUPS)
        piece_copy(g, z).wait_send()
        part_copy(0, g, z, j).wait_send()
        part_copy(1, g, z, j).wait_send()

    each(1, GROUPS, sent_group)
    part_copy(1 - j, z, z, j).wait_send()

    def sent_chip(d):
        chip = lax.rem(p + d, CHIPS)
        gather_copy(chip, p).wait_send()
        window_copy(chip, p).wait_send()
        stat_copy(chip).wait_send()
        total_copy(chip, p).wait_send()
        kv_copy(chip % 8, chip // 8).wait_send()

    each(1, CHIPS, sent_chip)
    each(0, 4, lambda n: fwd_copy(n, j).wait_send())

    def sent_slot(k):
        @pl.when(k != slot)
        def _():
            qt_copy(k).wait_send()
            dec_copy(k).wait_send()

    each(0, 8, sent_slot)


def on_device(
    window_states,
    query_weight,
    cache_keys,
    cache_values,
    kept_blocks,
    retained_block_count,
    decode_queries,
    tail_keys,
    tail_values,
    row_lengths,
):
    cosine, sine = rotary_table()
    queries = (
        decode_queries.reshape(STEPS, KEY_HEADS, 8, HEAD_DIMENSION)
        .transpose(1, 0, 2, 3)
        .reshape(KEY_HEADS, 32, HEAD_DIMENSION)
    )
    hbm = pl.BlockSpec(memory_space=pl.ANY)
    smem = pl.BlockSpec(memory_space=pltpu.SMEM)
    vmem = pl.BlockSpec(memory_space=pltpu.VMEM)
    dma = pltpu.SemaphoreType.DMA
    votes, decoded = pl.pallas_call(
        body,
        out_shape=(
            jax.ShapeDtypeStruct((KEY_HEADS, POSITIONS), F32),
            jax.ShapeDtypeStruct((KEY_HEADS, 32, HEAD_DIMENSION), BF16),
        ),
        in_specs=[hbm, hbm, hbm, hbm, smem, smem, hbm, hbm, hbm, smem, vmem, vmem],
        out_specs=(vmem, vmem),
        scratch_shapes=[
            pltpu.VMEM((2, 1024, 256), BF16),
            pltpu.VMEM((POSITIONS, 1024), BF16),
            pltpu.VMEM((POSITIONS, 1024), BF16),
            pltpu.VMEM((ROWS, 1024), BF16),
            pltpu.VMEM((CHIPS, GROUPS, 16, 128), BF16),
            pltpu.VMEM((2, GROUPS, 32, 256), F32),
            pltpu.VMEM((GROUPS, 2, 32, 256), F32),
            pltpu.VMEM((CHIPS, 2, WIN, 128), BF16),
            pltpu.VMEM((KEY_HEADS, ROWS, 256), F32),
            pltpu.VMEM((CHIPS, 2, 128), F32),
            pltpu.VMEM((CHIPS, 2, 128), F32),
            pltpu.VMEM((2, 128), F32),
            pltpu.VMEM((CHIPS, 2, 128), F32),
            pltpu.VMEM((ROWS + 96, 128), F32),
            pltpu.VMEM((2, KEY_HEADS, POSITIONS), F32),
            pltpu.VMEM((KEY_HEADS, POSITIONS), F32),
            pltpu.VMEM((KEY_HEADS, KV_ROWS, 128), BF16),
            pltpu.VMEM((2 * CHIPS, KV_ROWS, 128), BF16),
            pltpu.VMEM((KEY_HEADS, QT_ROWS, 128), BF16),
            pltpu.VMEM((8, QT_ROWS, 128), BF16),
            pltpu.VMEM((2 * CHIPS, 256, 128), F32),
            pltpu.VMEM((8, 32, 128), F32),
            pltpu.VMEM((8, 32, 128), BF16),
            pltpu.VMEM((8, 32, 128), BF16),
            dma((32,)),
            dma((GROUPS,)),
            dma((GROUPS,)),
            dma((CHIPS,)),
            dma((CHIPS,)),
            dma((5,)),
            dma((5,)),
            dma((2, GROUPS)),
            dma((GROUPS, 2)),
            dma((CHIPS,)),
            dma((CHIPS,)),
            dma((CHIPS,)),
            dma((CHIPS,)),
            dma((CHIPS,)),
            dma((CHIPS,)),
            dma((CHIPS,)),
            dma((CHIPS,)),
            dma((4,)),
            dma((4,)),
            dma((8,)),
            dma((8,)),
            dma((8,)),
            dma((8,)),
        ],
        compiler_params=pltpu.CompilerParams(
            collective_id=0, has_side_effects=True, vmem_limit_bytes=48 * 1024 * 1024
        ),
        cost_estimate=pl.CostEstimate(
            flops=1_400_000_000, bytes_accessed=6_000_000, transcendentals=3_500_000
        ),
    )(
        window_states,
        query_weight,
        cache_keys,
        cache_values,
        kept_blocks,
        retained_block_count,
        queries,
        tail_keys,
        tail_values,
        row_lengths,
        jnp.asarray(cosine),
        jnp.asarray(sine),
    )
    decoded = (
        decoded.reshape(KEY_HEADS, STEPS, 8, HEAD_DIMENSION)
        .transpose(1, 0, 2, 3)
        .reshape(1, STEPS, 1, KEY_HEADS * 8 * HEAD_DIMENSION)
    )
    return votes[None], decoded


def solution(mesh):
    placed = (
        P("grp", None, None),
        P("grp", "ctx"),
        P("grp", "ctx", None),
        P("grp", "ctx", None),
        P("grp", None, "ctx"),
        P("grp", None, "ctx"),
        P("grp", None, "ctx", None),
        P("grp", "ctx", None, None),
        P("grp", "ctx", None, None),
        P("grp", "ctx"),
    )
    return jax.shard_map(
        on_device,
        mesh=mesh,
        in_specs=placed,
        out_specs=(P("grp", None, "ctx"), P("grp", None, "ctx", None)),
        check_vma=False,
    )
```

```python
import math

import jax
import jax.numpy as jnp
import numpy as np
from jax import lax
from jax.experimental import pallas as pl
from jax.experimental.pallas import tpu as pltpu
from jax.sharding import PartitionSpec as P

MESH = pl.DeviceIdType.MESH
F32 = jnp.float32
BF16 = jnp.bfloat16
KEY_HEADS = 8
HEAD_DIMENSION = 128
BLOCK = 128
POOL = 7
WIN = 64
STEPS = 4
CHIPS = 16
GROUPS = 8
PAIRS = GROUPS // 2
POSITIONS = 512
SPAN = 2 * POSITIONS
EDGE = 16
ROWS = SPAN + 2 * EDGE
PIECE = 96
NPIECE = ROWS // PIECE
KV_ROWS = 2 * BLOCK + 16
QT_ROWS = 192
LOW = -1e30
SCALE = 1.0 / math.sqrt(HEAD_DIMENSION)
NT = (((1,), (1,)), ((), ()))


def rotary_table():
    exponent = np.arange(0, HEAD_DIMENSION, 2).astype(np.float32) / np.float32(HEAD_DIMENSION)
    inverse = np.power(np.float32(500000.0), -exponent).astype(np.float32)
    wavelength = np.float32(2.0 * math.pi) / inverse
    smooth = (np.float32(8192.0) / wavelength - np.float32(1.0)) / np.float32(3.0)
    blended = (np.float32(1.0) - smooth) * inverse / np.float32(8.0) + smooth * inverse
    adjusted = np.where(
        wavelength > 8192.0,
        inverse / np.float32(8.0),
        np.where(wavelength < 2048.0, inverse, blended),
    ).astype(np.float32)
    start = 2 * CHIPS * POSITIONS - WIN
    positions = (np.arange(WIN) + start).astype(np.float32)
    angles = (positions[:, None] * adjusted[None, :]).astype(np.float32).astype(np.float64)
    cosine, sine = np.cos(angles), np.sin(angles)
    return np.stack(
        [np.concatenate([cosine, cosine], axis=1), np.concatenate([-sine, sine], axis=1)]
    ).astype(np.float32)


def dot(a, b):
    return jnp.dot(a, b, preferred_element_type=F32)


def dot_nt(a, b):
    return lax.dot_general(a, b, NT, preferred_element_type=F32)


def body(
    states,
    weight,
    keys,
    values,
    kept,
    counts,
    queries,
    tail_keys,
    tail_values,
    lengths,
    turn,
    votes_out,
    decode_out,
    w_all,
    keys_own,
    values_own,
    keys_span,
    gathered,
    partial,
    parts,
    window,
    exps,
    stat,
    stat_in,
    columns,
    pooled,
    pooled_in,
    kv_out,
    kv_in,
    qt_out,
    qt_in,
    dec_scores,
    tail_scores,
    dec_send,
    dec_in,
    kept_own,
    counts_own,
    lengths_own,
    turn_own,
    queries_own,
    local_sem,
    piece_send,
    piece_recv,
    gather_send,
    gather_recv,
    pair_send,
    pair_recv,
    part_send,
    part_recv,
    window_send,
    window_recv,
    stat_send,
    stat_recv,
    weight_send,
    weight_recv,
    kv_send,
    kv_recv,
    fwd_send,
    fwd_recv,
    qt_send,
    qt_recv,
    dec_send_sem,
    dec_recv,
):
    c = lax.axis_index("ctx")
    z = lax.axis_index("grp")
    p = c // 2
    j = c % 2
    sibling = 2 * p + (1 - j)
    half = p // 8
    slot = p % 8

    def remote(src, dst, send_sem, recv_sem, ctx, grp):
        return pltpu.make_async_remote_copy(
            src_ref=src,
            dst_ref=dst,
            send_sem=send_sem,
            recv_sem=recv_sem,
            device_id=(ctx, grp),
            device_id_type=MESH,
        )

    def core_of(chip):
        return 2 * chip + j

    def each(low, high, step):
        def go(i, carry):
            step(i)
            return carry

        lax.fori_loop(low, high, go, 0)

    def every(low, high, step):
        for i in range(low, high):
            step(i)

    side = z % 2
    pair = z // 2
    other = 2 * pair + 1 - side

    barrier = pltpu.get_barrier_semaphore()

    def greet(ctx, grp):
        pl.semaphore_signal(barrier, inc=1, device_id=(ctx, grp), device_id_type=MESH)

    def group_of(d):
        return 2 * lax.rem(pair + d, PAIRS) + side

    for d in range(1, PAIRS):
        greet(c, group_of(d))
        greet(sibling, group_of(d))
    greet(c, other)
    greet(sibling, z)
    every(1, CHIPS, lambda d: greet(core_of(lax.rem(p + d, CHIPS)), z))

    own_rows = pl.ds(pl.multiple_of(EDGE + j * POSITIONS, 16), POSITIONS)
    load_w = pltpu.make_async_copy(weight, w_all.at[side, j], local_sem.at[0])
    load_k = pltpu.make_async_copy(keys.at[0], keys_own, local_sem.at[1])
    load_v = pltpu.make_async_copy(values.at[0], values_own, local_sem.at[2])
    load_span = pltpu.make_async_copy(keys.at[0], keys_span.at[own_rows], local_sem.at[3])
    row0 = pl.multiple_of(32 * j + 16 * (p // 8), 16)

    def piece_of(q):
        col0 = pl.multiple_of(q * 2048 + 256 * (p % 8), 256)
        return states.at[0, pl.ds(row0, 16), pl.ds(col0, 256)]

    load_piece = pltpu.make_async_copy(piece_of(pair), gathered.at[p, pair], local_sem.at[4])
    small = [
        pltpu.make_async_copy(src, dst, local_sem.at[32 + n])
        for n, (src, dst) in enumerate(
            (
                (kept, kept_own),
                (counts, counts_own),
                (lengths, lengths_own),
                (turn, turn_own),
                (queries, queries_own),
            )
        )
    ]

    def qt_load(k):
        cols = slice(k * 128, (k + 1) * 128)
        return (
            pltpu.make_async_copy(
                tail_keys.at[0, 0, :, cols], qt_out.at[k, 0:64], local_sem.at[8 + k]
            ),
            pltpu.make_async_copy(
                tail_values.at[0, 0, :, cols], qt_out.at[k, 64:128], local_sem.at[16 + k]
            ),
        )

    load_k.start()
    load_v.start()
    for copy in small:
        copy.start()
    load_piece.start()
    load_w.start()
    load_span.start()
    for k in range(KEY_HEADS):
        for copy in qt_load(k):
            copy.start()

    for copy in small:
        copy.wait()
    load_k.wait()
    load_v.wait()
    for k in range(KEY_HEADS):
        cols = slice(k * 128, (k + 1) * 128)
        block = jnp.broadcast_to(kept_own[:, k : k + 1], (BLOCK, 128)) - c * (POSITIONS // BLOCK)
        chosen = [
            jnp.where(block == b, 1.0, 0.0).astype(BF16) for b in range(POSITIONS // BLOCK)
        ]
        for n, own in ((0, keys_own), (1, values_own)):
            kv_out[k, n * BLOCK : (n + 1) * BLOCK, :] = sum(
                chosen[b] * own[b * BLOCK : (b + 1) * BLOCK, cols]
                for b in range(POSITIONS // BLOCK)
            )
        live = jnp.broadcast_to(counts_own[:, k : k + 1], (16, 128)) > 0
        kv_out[k, 2 * BLOCK : KV_ROWS, :] = jnp.where(live, 0.0, LOW).astype(BF16)
    step_row = lax.broadcasted_iota(jnp.int32, (32, 128), 0) // 8
    lane = lax.broadcasted_iota(jnp.int32, (32, 128), 1)
    tail_bias = jnp.where(
        lane < jnp.broadcast_to(lengths_own[...], (32, 128)) + step_row, 0.0, LOW
    ).astype(BF16)
    for k in range(KEY_HEADS):
        qt_out[k, 128:160, :] = queries_own[k]
        qt_out[k, 160:QT_ROWS, :] = tail_bias

    pl.semaphore_wait(barrier, CHIPS - 1 + 1 + 2 * (PAIRS - 1) + 1)

    def piece_copy(q_to, q_from):
        return remote(
            piece_of(q_to),
            gathered.at[p, q_from],
            piece_send.at[q_to],
            piece_recv.at[q_from],
            c,
            2 * q_to + side,
        )

    def pair_before(d):
        return lax.rem(pair + PAIRS - d, PAIRS)

    every(1, PAIRS, lambda d: piece_copy(lax.rem(pair + d, PAIRS), pair).start())

    def weight_copy(n):
        rows = pl.ds(512 * n, 512)
        return remote(
            weight.at[rows],
            w_all.at[side, j, rows],
            weight_send.at[n],
            weight_recv.at[n],
            c,
            other,
        )

    def weight_on(n):
        part = w_all.at[1 - side, j, pl.ds(512 * n, 512)]
        return remote(part, part, weight_send.at[2 + n], weight_recv.at[2 + n], sibling, z)

    share_w = remote(weight, w_all.at[side, j], pair_send.at[0], pair_recv.at[0], sibling, z)
    share_k = remote(keys.at[0], keys_span.at[own_rows], pair_send.at[1], pair_recv.at[1], sibling, z)
    weight_copy(0).start()
    weight_copy(1).start()
    share_w.start()

    load_piece.wait()
    every(1, PAIRS, lambda d: piece_copy(pair_before(d), pair_before(d)).wait_recv())

    def gather_copy(chip, source):
        return remote(
            gathered.at[source],
            gathered.at[source],
            gather_send.at[chip],
            gather_recv.at[source],
            core_of(chip),
            z,
        )

    every(1, CHIPS, lambda d: gather_copy(lax.rem(p + d, CHIPS), p).start())
    share_k.start()

    def kv_copy(k, half_to):
        chip = k + 8 * half_to
        return remote(
            kv_out.at[k],
            kv_in.at[j * CHIPS + p],
            kv_send.at[chip],
            kv_recv.at[p],
            core_of(chip),
            z,
        )

    def kv_go(d):
        chip = lax.rem(p + d, CHIPS)
        kv_copy(chip % 8, chip // 8).start()

    kv_self = pltpu.make_async_copy(kv_out.at[slot], kv_in.at[j * CHIPS + p], local_sem.at[5])
    kv_self.start()

    def qt_copy(k):
        return remote(
            qt_out.at[k],
            qt_in.at[slot],
            qt_send.at[k],
            qt_recv.at[slot],
            core_of(8 * half + k),
            z,
        )

    for k in range(KEY_HEADS):
        for copy in qt_load(k):
            copy.wait()

    qt_self = pltpu.make_async_copy(qt_out.at[slot], qt_in.at[slot], local_sem.at[6])
    qt_self.start()

    every(1, CHIPS, kv_go)

    def qt_go(k):
        @pl.when(k != slot)
        def _():
            qt_copy(k).start()

    every(0, KEY_HEADS, qt_go)

    load_w.wait()
    share_w.wait_recv()
    every(
        1,
        CHIPS,
        lambda d: gather_copy(
            lax.rem(p + CHIPS - d, CHIPS), lax.rem(p + CHIPS - d, CHIPS)
        ).wait_recv(),
    )

    def left_of(m):
        return jnp.concatenate(
            [gathered[m].reshape(64, 256), gathered[8 + m].reshape(64, 256)], axis=0
        )

    def product(core, group_side):
        acc = jnp.zeros((128, 256), F32)
        for m in range(4):
            acc = acc + dot(
                left_of(4 * group_side + m), w_all[group_side, core, 256 * m : 256 * (m + 1), :]
            )
        return acc

    for n in range(2):
        weight_copy(n).wait_recv()
        weight_on(n).start()
    for n in range(2):
        weight_on(n).wait_recv()
    for core in range(2):
        acc = (product(core, 0) + product(core, 1)).reshape(2, PAIRS, 16, 256)
        for i in range(2):
            partial[core, :, 16 * i : 16 * (i + 1), :] = acc[i]

    def part_copy(core, q_to, q_from, j_from):
        return remote(
            partial.at[core, q_to],
            parts.at[q_from, j_from],
            part_send.at[core, q_to],
            part_recv.at[q_from, j_from],
            2 * p + core,
            2 * q_to + side,
        )

    for d in range(1, PAIRS):
        q = lax.rem(pair + d, PAIRS)
        part_copy(0, q, pair, j).start()
        part_copy(1, q, pair, j).start()
    part_copy(1 - j, pair, pair, j).start()
    parts[pair, j] = partial[j, pair]

    load_span.wait()
    share_k.wait_recv()

    def edge_copy(up):
        src = keys_span.at[pl.ds(SPAN if up else EDGE, EDGE)]
        dst = keys_span.at[pl.ds(0 if up else SPAN + EDGE, EDGE)]
        chip = p + 1 if up else p - 1
        n = 2 + int(up)
        return remote(src, dst, pair_send.at[n], pair_recv.at[n], core_of(chip), z)

    @pl.when(p < CHIPS - 1)
    def _():
        edge_copy(True).start()

    @pl.when(p > 0)
    def _():
        edge_copy(False).start()

    @pl.when(p == 0)
    def _():
        keys_span[0:EDGE, :] = jnp.zeros((EDGE, 1024), BF16)

    @pl.when(p == CHIPS - 1)
    def _():
        keys_span[SPAN + EDGE : ROWS, :] = jnp.zeros((EDGE, 1024), BF16)

    for d in range(1, PAIRS):
        part_copy(0, pair_before(d), pair_before(d), 0).wait_recv()
        part_copy(0, pair_before(d), pair_before(d), 1).wait_recv()
    part_copy(0, pair, pair, 1 - j).wait_recv()
    for i in range(2):
        summed = parts[0, i]
        for q in range(1, PAIRS):
            summed = summed + parts[q, i]
        turn_c = turn_own[0, 32 * i : 32 * (i + 1), :]
        turn_s = turn_own[1, 32 * i : 32 * (i + 1), :]
        for h in range(2):
            head = summed[:, 128 * h : 128 * (h + 1)]
            turned = head * turn_c + pltpu.roll(head, 64, axis=1) * turn_s
            window[p, h, 32 * i : 32 * (i + 1), :] = turned.astype(BF16)

    def window_copy(chip, source):
        return remote(
            window.at[source],
            window.at[source],
            window_send.at[chip],
            window_recv.at[source],
            core_of(chip),
            z,
        )

    every(1, CHIPS, lambda d: window_copy(lax.rem(p + d, CHIPS), p).start())

    kv_self.wait()

    def kv_wait(source):
        @pl.when(source != p)
        def _():
            remote(
                kv_in.at[j * CHIPS + source],
                kv_in.at[j * CHIPS + source],
                kv_send.at[0],
                kv_recv.at[source],
                core_of(source),
                z,
            ).wait_recv()

    def fwd_copy(n, core):
        part = kv_in.at[pl.ds(core * CHIPS + 4 * n, 4)]
        return remote(part, part, fwd_send.at[n], fwd_recv.at[n], sibling, z)

    for n in range(4):
        every(4 * n, 4 * n + 4, kv_wait)
        fwd_copy(n, j).start()


    @pl.when(p > 0)
    def _():
        edge_copy(True).wait_recv()

    @pl.when(p < CHIPS - 1)
    def _():
        edge_copy(False).wait_recv()

    piece_row = lax.broadcasted_iota(jnp.int32, (PIECE, 256), 0)
    piece_lane = lax.broadcasted_iota(jnp.int32, (PIECE, 256), 1)
    hidden_first = jnp.logical_and(piece_row < EDGE, p == 0)
    last_row = piece_row + (NPIECE - 1) * PIECE
    hidden_last = jnp.logical_or(
        jnp.logical_and(last_row >= SPAN + EDGE, p == CHIPS - 1),
        jnp.logical_and(
            last_row < SPAN + EDGE,
            p * SPAN + last_row - EDGE
            > (2 * CHIPS * POSITIONS - WIN) + jnp.bitwise_and(piece_lane, WIN - 1),
        ),
    )

    def stat_copy(chip, source):
        return remote(
            stat, stat_in.at[source], stat_send.at[chip], stat_recv.at[source], core_of(chip), z
        )

    stat_row = lax.broadcasted_iota(jnp.int32, (CHIPS, 128), 0)

    def window_go(k, carry):
        tops, sums = carry
        for n in range(2):
            source = 2 * k + n

            @pl.when(source != p)
            def _():
                window_copy(0, source).wait_recv()

        rows = window[pl.ds(2 * k, 2)].reshape(256, 128)
        cols = pl.ds(pl.multiple_of(k * 128, 128), 128)
        top = jnp.full((8, 256), LOW, F32)
        for i in range(NPIECE):
            s = dot_nt(keys_span[PIECE * i : PIECE * (i + 1), cols], rows) * SCALE
            if i == 0:
                s = jnp.where(hidden_first, LOW, s)
            if i == NPIECE - 1:
                s = jnp.where(hidden_last, LOW, s)
            exps[k, PIECE * i : PIECE * (i + 1), :] = s
            top = jnp.maximum(top, jnp.max(s.reshape(PIECE // 8, 8, 256), axis=0))
        top = jnp.max(top, axis=0, keepdims=True)
        summed = jnp.zeros((8, 256), F32)
        for i in range(NPIECE):
            e = jnp.exp(exps[k, PIECE * i : PIECE * (i + 1), :] - top)
            exps[k, PIECE * i : PIECE * (i + 1), :] = e
            if i == 0:
                e = e[EDGE:]
            if i == NPIECE - 1:
                e = e[: PIECE - EDGE]
            summed = summed + jnp.sum(e.reshape(-1, 8, 256), axis=0)
        summed = jnp.sum(summed, axis=0, keepdims=True)
        for n in range(2):
            here = stat_row == 2 * k + n
            tops = jnp.where(here, top[:, 128 * n : 128 * (n + 1)], tops)
            sums = jnp.where(here, summed[:, 128 * n : 128 * (n + 1)], sums)
        return tops, sums

    tops, sums = lax.fori_loop(
        0, KEY_HEADS, window_go, (jnp.zeros((CHIPS, 128), F32), jnp.zeros((CHIPS, 128), F32))
    )
    stat[0] = tops
    stat[1] = sums
    every(1, CHIPS, lambda d: stat_copy(lax.rem(p + d, CHIPS), p).start())
    stat_in[p] = stat[...]

    qt_self.wait()

    def qt_wait(r):
        @pl.when(r != slot)
        def _():
            remote(
                qt_in.at[r], qt_in.at[r], qt_send.at[0], qt_recv.at[r], core_of(8 * half + r), z
            ).wait_recv()

    every(0, 8, qt_wait)
    every(0, 4, lambda n: fwd_copy(n, 1 - j).wait_recv())
    rows_q = qt_in[:, 128:160, :].reshape(256, 128)

    def tail_go(r):
        s = dot_nt(qt_in[r, 128:160, :], qt_in[r, 0:128, :]) * SCALE
        tail_scores[r] = s + qt_in[r, 160:QT_ROWS, :].astype(F32)

    each(0, 8, tail_go)
    top = tail_scores[...].reshape(256, 128)

    def score_go(n, top):
        right = kv_in[pl.ds(4 * n, 4), 0:BLOCK, :].reshape(4 * BLOCK, 128)
        s = dot_nt(rows_q, right) * SCALE
        for i in range(4):
            bias = kv_in[4 * n + i, 2 * BLOCK : KV_ROWS, :].astype(F32)[0:1, :]
            one = s[:, BLOCK * i : BLOCK * (i + 1)] + bias
            dec_scores[n, :, BLOCK * i : BLOCK * (i + 1)] = one
            top = jnp.maximum(top, one)
        return top

    top = lax.fori_loop(0, CHIPS // 2, score_go, top)
    top = jnp.max(top, axis=1, keepdims=True)

    def split(weights):
        high = weights.astype(BF16)
        return high, (weights - high.astype(F32)).astype(BF16)

    tail_weights = jnp.exp(tail_scores[...].reshape(256, 128) - top)
    tail_acc = []
    for r in range(8):
        high, low = split(tail_weights[32 * r : 32 * (r + 1), :])
        right = qt_in[r, 64:QT_ROWS, :]
        tail_acc.append(dot(high, right) + dot(low, right))

    def value_go(n, carry):
        acc, weight_sum = carry
        weights = jnp.exp(dec_scores[n] - top)
        high, low = split(weights)
        right = kv_in[pl.ds(4 * n, 4), BLOCK : 2 * BLOCK, :].reshape(4 * BLOCK, 128)
        for i in range(4):
            weight_sum = weight_sum + weights[:, BLOCK * i : BLOCK * (i + 1)]
        return acc + (dot(high, right) + dot(low, right)), weight_sum

    acc, weight_sum = lax.fori_loop(
        0, CHIPS // 2, value_go, (jnp.concatenate(tail_acc, axis=0), tail_weights)
    )
    result = acc / jnp.sum(weight_sum, axis=1, keepdims=True)
    dec_send[...] = result.astype(BF16).reshape(8, 32, 128)

    def dec_copy(r):
        return remote(
            dec_send.at[r],
            dec_in.at[slot],
            dec_send_sem.at[r],
            dec_recv.at[slot],
            core_of(8 * half + r),
            z,
        )

    def dec_go(r):
        @pl.when(r != slot)
        def _():
            dec_copy(r).start()

    every(0, 8, dec_go)
    dec_self = pltpu.make_async_copy(dec_send.at[slot], dec_in.at[slot], local_sem.at[7])
    dec_self.start()

    every(
        1,
        CHIPS,
        lambda d: stat_copy(
            lax.rem(p + CHIPS - d, CHIPS), lax.rem(p + CHIPS - d, CHIPS)
        ).wait_recv(),
    )
    peak = stat_in[0, 0]
    for o in range(1, CHIPS):
        peak = jnp.maximum(peak, stat_in[o, 0])
    merged = jnp.zeros((CHIPS, 128), F32)
    for o in range(CHIPS):
        merged = merged + stat_in[o, 1] * jnp.exp(stat_in[o, 0] - peak)
    factor = jnp.exp(stat[0] - peak) / merged

    factors = [factor[o : o + 1, :] for o in range(CHIPS)]
    head_lane = lax.broadcasted_iota(jnp.int32, (PIECE, 128), 1)
    for i in range(NPIECE):
        rows = slice(PIECE * i, PIECE * (i + 1))
        votes = jnp.zeros((PIECE, 128), F32)
        for k in range(KEY_HEADS):
            weighted = (
                exps[k, rows, 0:128] * factors[2 * k] + exps[k, rows, 128:256] * factors[2 * k + 1]
            )
            votes = jnp.where(head_lane == k, jnp.sum(weighted, axis=1, keepdims=True), votes)
        columns[rows, :] = votes
    columns[ROWS:, :] = jnp.zeros((columns.shape[0] - ROWS, 128), F32)
    lanes = columns.shape[0]
    across = jnp.transpose(columns[...])[0:KEY_HEADS, :]
    near = POOL // 2
    window_sum = jnp.zeros((KEY_HEADS, lanes), F32)
    for shift in range(EDGE - near, EDGE + near + 1):
        window_sum = window_sum + pltpu.roll(across, lanes - shift, axis=1)
    for n in range(2):
        pooled[n] = window_sum[:, POSITIONS * n : POSITIONS * (n + 1)]
    share_votes = remote(pooled.at[1 - j], pooled_in, pair_send.at[4], pair_recv.at[4], sibling, z)
    share_votes.start()

    dec_self.wait()

    def dec_wait(k):
        @pl.when(k != slot)
        def _():
            remote(
                dec_send.at[k], dec_in.at[k], dec_send_sem.at[0], dec_recv.at[k], core_of(8 * half + k), z
            ).wait_recv()

    every(0, 8, dec_wait)
    decode_out[...] = dec_in[...]

    share_votes.wait_recv()
    votes_out[...] = (pooled[j] + pooled_in[...]) * (
        2 * CHIPS * POSITIONS / (WIN * 8) / POOL
    )

    share_votes.wait_send()
    share_w.wait_send()
    share_k.wait_send()

    @pl.when(p < CHIPS - 1)
    def _():
        edge_copy(True).wait_send()

    @pl.when(p > 0)
    def _():
        edge_copy(False).wait_send()

    for d in range(1, PAIRS):
        q = lax.rem(pair + d, PAIRS)
        piece_copy(q, pair).wait_send()
        part_copy(0, q, pair, j).wait_send()
        part_copy(1, q, pair, j).wait_send()
    part_copy(1 - j, pair, pair, j).wait_send()
    for n in range(2):
        weight_copy(n).wait_send()
        weight_on(n).wait_send()

    def sent_chip(d):
        chip = lax.rem(p + d, CHIPS)
        gather_copy(chip, p).wait_send()
        window_copy(chip, p).wait_send()
        stat_copy(chip, p).wait_send()
        kv_copy(chip % 8, chip // 8).wait_send()

    each(1, CHIPS, sent_chip)
    each(0, 4, lambda n: fwd_copy(n, j).wait_send())

    def sent_slot(k):
        @pl.when(k != slot)
        def _():
            qt_copy(k).wait_send()
            dec_copy(k).wait_send()

    each(0, 8, sent_slot)


def on_device(
    window_states,
    query_weight,
    cache_keys,
    cache_values,
    kept_blocks,
    retained_block_count,
    decode_queries,
    tail_keys,
    tail_values,
    row_lengths,
):
    queries = (
        decode_queries.reshape(STEPS, KEY_HEADS, 8, HEAD_DIMENSION)
        .transpose(1, 0, 2, 3)
        .reshape(KEY_HEADS, 32, HEAD_DIMENSION)
    )
    hbm = pl.BlockSpec(memory_space=pl.ANY)
    vmem = pl.BlockSpec(memory_space=pltpu.VMEM)
    dma = pltpu.SemaphoreType.DMA
    votes, decoded = pl.pallas_call(
        body,
        out_shape=(
            jax.ShapeDtypeStruct((KEY_HEADS, POSITIONS), F32),
            jax.ShapeDtypeStruct((KEY_HEADS, 32, HEAD_DIMENSION), BF16),
        ),
        in_specs=[hbm] * 11,
        out_specs=(vmem, vmem),
        scratch_shapes=[
            pltpu.VMEM((2, 2, 1024, 256), BF16),
            pltpu.VMEM((POSITIONS, 1024), BF16),
            pltpu.VMEM((POSITIONS, 1024), BF16),
            pltpu.VMEM((ROWS, 1024), BF16),
            pltpu.VMEM((CHIPS, PAIRS, 16, 256), BF16),
            pltpu.VMEM((2, PAIRS, 32, 256), F32),
            pltpu.VMEM((PAIRS, 2, 32, 256), F32),
            pltpu.VMEM((CHIPS, 2, WIN, 128), BF16),
            pltpu.VMEM((KEY_HEADS, ROWS, 256), F32),
            pltpu.VMEM((2, CHIPS, 128), F32),
            pltpu.VMEM((CHIPS, 2, CHIPS, 128), F32),
            pltpu.VMEM((ROWS + 96, 128), F32),
            pltpu.VMEM((2, KEY_HEADS, POSITIONS), F32),
            pltpu.VMEM((KEY_HEADS, POSITIONS), F32),
            pltpu.VMEM((KEY_HEADS, KV_ROWS, 128), BF16),
            pltpu.VMEM((2 * CHIPS, KV_ROWS, 128), BF16),
            pltpu.VMEM((KEY_HEADS, QT_ROWS, 128), BF16),
            pltpu.VMEM((8, QT_ROWS, 128), BF16),
            pltpu.VMEM((CHIPS // 2, 256, 4 * BLOCK), F32),
            pltpu.VMEM((8, 32, 128), F32),
            pltpu.VMEM((8, 32, 128), BF16),
            pltpu.VMEM((8, 32, 128), BF16),
            pltpu.VMEM((1, 8), jnp.int32),
            pltpu.VMEM((1, 8), jnp.int32),
            pltpu.VMEM((1, 1), jnp.int32),
            pltpu.VMEM((2, WIN, 128), F32),
            pltpu.VMEM((KEY_HEADS, 32, 128), BF16),
            dma((40,)),
            dma((PAIRS,)),
            dma((PAIRS,)),
            dma((CHIPS,)),
            dma((CHIPS,)),
            dma((5,)),
            dma((5,)),
            dma((2, PAIRS)),
            dma((PAIRS, 2)),
            dma((CHIPS,)),
            dma((CHIPS,)),
            dma((CHIPS,)),
            dma((CHIPS,)),
            dma((4,)),
            dma((4,)),
            dma((CHIPS,)),
            dma((CHIPS,)),
            dma((4,)),
            dma((4,)),
            dma((8,)),
            dma((8,)),
            dma((8,)),
            dma((8,)),
        ],
        compiler_params=pltpu.CompilerParams(
            collective_id=0, has_side_effects=True, vmem_limit_bytes=60 * 1024 * 1024
        ),
        cost_estimate=pl.CostEstimate(
            flops=1_400_000_000, bytes_accessed=6_000_000, transcendentals=3_500_000
        ),
    )(
        window_states,
        query_weight,
        cache_keys,
        cache_values,
        kept_blocks.reshape(1, KEY_HEADS),
        retained_block_count.reshape(1, KEY_HEADS),
        queries,
        tail_keys,
        tail_values,
        row_lengths,
        jnp.asarray(rotary_table()),
    )
    decoded = (
        decoded.reshape(KEY_HEADS, STEPS, 8, HEAD_DIMENSION)
        .transpose(1, 0, 2, 3)
        .reshape(1, STEPS, 1, KEY_HEADS * 8 * HEAD_DIMENSION)
    )
    return votes[None], decoded


def solution(mesh):
    placed = (
        P("grp", None, None),
        P("grp", "ctx"),
        P("grp", "ctx", None),
        P("grp", "ctx", None),
        P("grp", None, "ctx"),
        P("grp", None, "ctx"),
        P("grp", None, "ctx", None),
        P("grp", "ctx", None, None),
        P("grp", "ctx", None, None),
        P("grp", "ctx"),
    )
    return jax.shard_map(
        on_device,
        mesh=mesh,
        in_specs=placed,
        out_specs=(P("grp", None, "ctx"), P("grp", None, "ctx", None)),
        check_vma=False,
    )
```

```python
import math

import jax
import jax.numpy as jnp
import numpy as np
from jax import lax
from jax.experimental import pallas as pl
from jax.experimental.pallas import tpu as pltpu
from jax.sharding import PartitionSpec as P

MESH = pl.DeviceIdType.MESH
F32 = jnp.float32
BF16 = jnp.bfloat16
KEY_HEADS = 8
HEAD_DIMENSION = 128
BLOCK = 128
POOL = 7
WIN = 64
STEPS = 4
CHIPS = 16
GROUPS = 8
PAIRS = GROUPS // 2
POSITIONS = 512
SPAN = 2 * POSITIONS
EDGE = 16
ROWS = SPAN + 2 * EDGE
PIECE = 96
NPIECE = ROWS // PIECE
KV_ROWS = 2 * BLOCK + 16
QT_ROWS = 192
LOW = -1e30
SCALE = 1.0 / math.sqrt(HEAD_DIMENSION)
NT = (((1,), (1,)), ((), ()))


def rotary_table():
    exponent = np.arange(0, HEAD_DIMENSION, 2).astype(np.float32) / np.float32(HEAD_DIMENSION)
    inverse = np.power(np.float32(500000.0), -exponent).astype(np.float32)
    wavelength = np.float32(2.0 * math.pi) / inverse
    smooth = (np.float32(8192.0) / wavelength - np.float32(1.0)) / np.float32(3.0)
    blended = (np.float32(1.0) - smooth) * inverse / np.float32(8.0) + smooth * inverse
    adjusted = np.where(
        wavelength > 8192.0,
        inverse / np.float32(8.0),
        np.where(wavelength < 2048.0, inverse, blended),
    ).astype(np.float32)
    start = 2 * CHIPS * POSITIONS - WIN
    positions = (np.arange(WIN) + start).astype(np.float32)
    angles = (positions[:, None] * adjusted[None, :]).astype(np.float32).astype(np.float64)
    cosine, sine = np.cos(angles), np.sin(angles)
    return np.stack(
        [np.concatenate([cosine, cosine], axis=1), np.concatenate([-sine, sine], axis=1)]
    ).astype(np.float32)


def dot(a, b):
    return jnp.dot(a, b, preferred_element_type=F32)


def dot_nt(a, b):
    return lax.dot_general(a, b, NT, preferred_element_type=F32)


def body(
    states,
    weight,
    keys,
    values,
    kept,
    counts,
    queries,
    tail_keys,
    tail_values,
    lengths,
    turn,
    votes_out,
    decode_out,
    w_all,
    keys_own,
    values_own,
    keys_span,
    gathered,
    partial,
    parts,
    window,
    exps,
    stat,
    stat_in,
    columns,
    pooled,
    pooled_in,
    kv_out,
    kv_in,
    qt_out,
    qt_in,
    dec_scores,
    tail_scores,
    dec_send,
    dec_in,
    kept_own,
    counts_own,
    lengths_own,
    turn_own,
    queries_own,
    rows_wide,
    local_sem,
    piece_send,
    piece_recv,
    gather_send,
    gather_recv,
    pair_send,
    pair_recv,
    part_send,
    part_recv,
    window_send,
    window_recv,
    stat_send,
    stat_recv,
    weight_send,
    weight_recv,
    kv_send,
    kv_recv,
    fwd_send,
    fwd_recv,
    qt_send,
    qt_recv,
    dec_send_sem,
    dec_recv,
):
    c = lax.axis_index("ctx")
    z = lax.axis_index("grp")
    p = c // 2
    j = c % 2
    sibling = 2 * p + (1 - j)
    half = p // 8
    slot = p % 8

    def remote(src, dst, send_sem, recv_sem, ctx, grp):
        return pltpu.make_async_remote_copy(
            src_ref=src,
            dst_ref=dst,
            send_sem=send_sem,
            recv_sem=recv_sem,
            device_id=(ctx, grp),
            device_id_type=MESH,
        )

    def core_of(chip):
        return 2 * chip + j

    def each(low, high, step):
        def go(i, carry):
            step(i)
            return carry

        lax.fori_loop(low, high, go, 0)

    def every(low, high, step):
        for i in range(low, high):
            step(i)

    side = z % 2
    pair = z // 2
    other = 2 * pair + 1 - side

    barrier = pltpu.get_barrier_semaphore()

    def greet(ctx, grp):
        pl.semaphore_signal(barrier, inc=1, device_id=(ctx, grp), device_id_type=MESH)

    def group_of(d):
        return 2 * lax.rem(pair + d, PAIRS) + side

    for d in range(1, PAIRS):
        greet(c, group_of(d))
        greet(sibling, group_of(d))
    greet(c, other)
    greet(sibling, z)
    every(1, CHIPS, lambda d: greet(core_of(lax.rem(p + d, CHIPS)), z))

    own_rows = pl.ds(pl.multiple_of(EDGE + j * POSITIONS, 16), POSITIONS)
    load_w = pltpu.make_async_copy(weight, w_all.at[side, j], local_sem.at[0])
    load_k = pltpu.make_async_copy(keys.at[0], keys_own, local_sem.at[1])
    load_v = pltpu.make_async_copy(values.at[0], values_own, local_sem.at[2])
    load_span = pltpu.make_async_copy(keys.at[0], keys_span.at[own_rows], local_sem.at[3])
    row0 = pl.multiple_of(32 * j + 16 * (p // 8), 16)

    def piece_of(q):
        col0 = pl.multiple_of(q * 2048 + 256 * (p % 8), 256)
        return states.at[0, pl.ds(row0, 16), pl.ds(col0, 256)]

    load_piece = pltpu.make_async_copy(piece_of(pair), gathered.at[p, pair], local_sem.at[4])
    small = [
        pltpu.make_async_copy(src, dst, local_sem.at[32 + n])
        for n, (src, dst) in enumerate(
            (
                (kept, kept_own),
                (counts, counts_own),
                (lengths, lengths_own),
                (turn, turn_own),
                (queries, queries_own),
            )
        )
    ]

    def qt_load(k):
        cols = slice(k * 128, (k + 1) * 128)
        return (
            pltpu.make_async_copy(
                tail_keys.at[0, 0, :, cols], qt_out.at[k, 0:64], local_sem.at[8 + k]
            ),
            pltpu.make_async_copy(
                tail_values.at[0, 0, :, cols], qt_out.at[k, 64:128], local_sem.at[16 + k]
            ),
        )

    load_k.start()
    load_v.start()
    for copy in small:
        copy.start()
    load_piece.start()
    load_w.start()
    load_span.start()
    for k in range(KEY_HEADS):
        for copy in qt_load(k):
            copy.start()

    for copy in small:
        copy.wait()
    load_k.wait()
    load_v.wait()
    for k in range(KEY_HEADS):
        cols = slice(k * 128, (k + 1) * 128)
        block = jnp.broadcast_to(kept_own[:, k : k + 1], (BLOCK, 128)) - c * (POSITIONS // BLOCK)
        chosen = [
            jnp.where(block == b, 1.0, 0.0).astype(BF16) for b in range(POSITIONS // BLOCK)
        ]
        for n, own in ((0, keys_own), (1, values_own)):
            kv_out[k, n * BLOCK : (n + 1) * BLOCK, :] = sum(
                chosen[b] * own[b * BLOCK : (b + 1) * BLOCK, cols]
                for b in range(POSITIONS // BLOCK)
            )
        live = jnp.broadcast_to(counts_own[:, k : k + 1], (16, 128)) > 0
        kv_out[k, 2 * BLOCK : KV_ROWS, :] = jnp.where(live, 0.0, LOW).astype(BF16)
    step_row = lax.broadcasted_iota(jnp.int32, (32, 128), 0) % STEPS
    lane = lax.broadcasted_iota(jnp.int32, (32, 128), 1)
    tail_bias = jnp.where(
        lane < jnp.broadcast_to(lengths_own[...], (32, 128)) + step_row, 0.0, LOW
    ).astype(BF16)
    for k in range(KEY_HEADS):
        for h in range(8):
            rows_wide[32 * k + 4 * h : 32 * k + 4 * (h + 1), :] = queries_own[8 * k + h].astype(F32)
        qt_out[k, 128:160, :] = rows_wide[32 * k : 32 * (k + 1), :].astype(BF16)
        qt_out[k, 160:QT_ROWS, :] = tail_bias

    pl.semaphore_wait(barrier, CHIPS - 1 + 1 + 2 * (PAIRS - 1) + 1)

    def piece_copy(q_to, q_from):
        return remote(
            piece_of(q_to),
            gathered.at[p, q_from],
            piece_send.at[q_to],
            piece_recv.at[q_from],
            c,
            2 * q_to + side,
        )

    def pair_before(d):
        return lax.rem(pair + PAIRS - d, PAIRS)

    every(1, PAIRS, lambda d: piece_copy(lax.rem(pair + d, PAIRS), pair).start())

    def weight_copy(n):
        rows = pl.ds(512 * n, 512)
        return remote(
            weight.at[rows],
            w_all.at[side, j, rows],
            weight_send.at[n],
            weight_recv.at[n],
            c,
            other,
        )

    def weight_on(n):
        part = w_all.at[1 - side, j, pl.ds(512 * n, 512)]
        return remote(part, part, weight_send.at[2 + n], weight_recv.at[2 + n], sibling, z)

    share_w = remote(weight, w_all.at[side, j], pair_send.at[0], pair_recv.at[0], sibling, z)
    share_k = remote(keys.at[0], keys_span.at[own_rows], pair_send.at[1], pair_recv.at[1], sibling, z)
    weight_copy(0).start()
    weight_copy(1).start()
    share_w.start()

    load_piece.wait()
    every(1, PAIRS, lambda d: piece_copy(pair_before(d), pair_before(d)).wait_recv())

    def gather_copy(chip, source):
        return remote(
            gathered.at[source],
            gathered.at[source],
            gather_send.at[chip],
            gather_recv.at[source],
            core_of(chip),
            z,
        )

    every(1, CHIPS, lambda d: gather_copy(lax.rem(p + d, CHIPS), p).start())
    share_k.start()

    def kv_copy(k, half_to):
        chip = k + 8 * half_to
        return remote(
            kv_out.at[k],
            kv_in.at[j * CHIPS + p],
            kv_send.at[chip],
            kv_recv.at[p],
            core_of(chip),
            z,
        )

    def kv_go(d):
        chip = lax.rem(p + d, CHIPS)
        kv_copy(chip % 8, chip // 8).start()

    kv_self = pltpu.make_async_copy(kv_out.at[slot], kv_in.at[j * CHIPS + p], local_sem.at[5])
    kv_self.start()

    def qt_copy(k):
        return remote(
            qt_out.at[k],
            qt_in.at[slot],
            qt_send.at[k],
            qt_recv.at[slot],
            core_of(8 * half + k),
            z,
        )

    for k in range(KEY_HEADS):
        for copy in qt_load(k):
            copy.wait()

    qt_self = pltpu.make_async_copy(qt_out.at[slot], qt_in.at[slot], local_sem.at[6])
    qt_self.start()

    load_w.wait()
    share_w.wait_recv()
    every(
        1,
        CHIPS,
        lambda d: gather_copy(
            lax.rem(p + CHIPS - d, CHIPS), lax.rem(p + CHIPS - d, CHIPS)
        ).wait_recv(),
    )

    every(1, CHIPS, kv_go)

    def qt_go(k):
        @pl.when(k != slot)
        def _():
            qt_copy(k).start()

    every(0, KEY_HEADS, qt_go)

    def left_of(m):
        return jnp.concatenate(
            [gathered[m].reshape(64, 256), gathered[8 + m].reshape(64, 256)], axis=0
        )

    def product(core, group_side):
        acc = jnp.zeros((128, 256), F32)
        for m in range(4):
            acc = acc + dot(
                left_of(4 * group_side + m), w_all[group_side, core, 256 * m : 256 * (m + 1), :]
            )
        return acc

    for n in range(2):
        weight_copy(n).wait_recv()
        weight_on(n).start()
    for n in range(2):
        weight_on(n).wait_recv()
    for core in range(2):
        acc = (product(core, 0) + product(core, 1)).reshape(2, PAIRS, 16, 256)
        for i in range(2):
            partial[core, :, 16 * i : 16 * (i + 1), :] = acc[i]

    def part_copy(core, q_to, q_from, j_from):
        return remote(
            partial.at[core, q_to],
            parts.at[q_from, j_from],
            part_send.at[core, q_to],
            part_recv.at[q_from, j_from],
            2 * p + core,
            2 * q_to + side,
        )

    for d in range(1, PAIRS):
        q = lax.rem(pair + d, PAIRS)
        part_copy(0, q, pair, j).start()
        part_copy(1, q, pair, j).start()
    part_copy(1 - j, pair, pair, j).start()
    parts[pair, j] = partial[j, pair]

    load_span.wait()
    share_k.wait_recv()

    def edge_copy(up):
        src = keys_span.at[pl.ds(SPAN if up else EDGE, EDGE)]
        dst = keys_span.at[pl.ds(0 if up else SPAN + EDGE, EDGE)]
        chip = p + 1 if up else p - 1
        n = 2 + int(up)
        return remote(src, dst, pair_send.at[n], pair_recv.at[n], core_of(chip), z)

    @pl.when(p < CHIPS - 1)
    def _():
        edge_copy(True).start()

    @pl.when(p > 0)
    def _():
        edge_copy(False).start()

    @pl.when(p == 0)
    def _():
        keys_span[0:EDGE, :] = jnp.zeros((EDGE, 1024), BF16)

    @pl.when(p == CHIPS - 1)
    def _():
        keys_span[SPAN + EDGE : ROWS, :] = jnp.zeros((EDGE, 1024), BF16)

    for d in range(1, PAIRS):
        part_copy(0, pair_before(d), pair_before(d), 0).wait_recv()
        part_copy(0, pair_before(d), pair_before(d), 1).wait_recv()
    part_copy(0, pair, pair, 1 - j).wait_recv()
    for i in range(2):
        summed = parts[0, i]
        for q in range(1, PAIRS):
            summed = summed + parts[q, i]
        turn_c = turn_own[0, 32 * i : 32 * (i + 1), :]
        turn_s = turn_own[1, 32 * i : 32 * (i + 1), :]
        for h in range(2):
            head = summed[:, 128 * h : 128 * (h + 1)]
            turned = head * turn_c + pltpu.roll(head, 64, axis=1) * turn_s
            window[p, h, 32 * i : 32 * (i + 1), :] = turned.astype(BF16)

    def window_copy(chip, source):
        return remote(
            window.at[source],
            window.at[source],
            window_send.at[chip],
            window_recv.at[source],
            core_of(chip),
            z,
        )

    every(1, CHIPS, lambda d: window_copy(lax.rem(p + d, CHIPS), p).start())

    kv_self.wait()

    def kv_wait(source):
        @pl.when(source != p)
        def _():
            remote(
                kv_in.at[j * CHIPS + source],
                kv_in.at[j * CHIPS + source],
                kv_send.at[0],
                kv_recv.at[source],
                core_of(source),
                z,
            ).wait_recv()

    def fwd_copy(n, core):
        part = kv_in.at[pl.ds(core * CHIPS + 4 * n, 4)]
        return remote(part, part, fwd_send.at[n], fwd_recv.at[n], sibling, z)

    for n in range(4):
        every(4 * n, 4 * n + 4, kv_wait)
        fwd_copy(n, j).start()


    @pl.when(p > 0)
    def _():
        edge_copy(True).wait_recv()

    @pl.when(p < CHIPS - 1)
    def _():
        edge_copy(False).wait_recv()

    piece_row = lax.broadcasted_iota(jnp.int32, (PIECE, 256), 0)
    piece_lane = lax.broadcasted_iota(jnp.int32, (PIECE, 256), 1)
    hidden_first = jnp.logical_and(piece_row < EDGE, p == 0)
    last_row = piece_row + (NPIECE - 1) * PIECE
    hidden_last = jnp.logical_or(
        jnp.logical_and(last_row >= SPAN + EDGE, p == CHIPS - 1),
        jnp.logical_and(
            last_row < SPAN + EDGE,
            p * SPAN + last_row - EDGE
            > (2 * CHIPS * POSITIONS - WIN) + jnp.bitwise_and(piece_lane, WIN - 1),
        ),
    )

    def stat_copy(chip, source):
        return remote(
            stat, stat_in.at[source], stat_send.at[chip], stat_recv.at[source], core_of(chip), z
        )

    stat_row = lax.broadcasted_iota(jnp.int32, (CHIPS, 128), 0)

    def window_go(k, carry):
        tops, sums = carry
        for n in range(2):
            source = 2 * k + n

            @pl.when(source != p)
            def _():
                window_copy(0, source).wait_recv()

        rows = window[pl.ds(2 * k, 2)].reshape(256, 128)
        cols = pl.ds(pl.multiple_of(k * 128, 128), 128)
        top = jnp.full((8, 256), LOW, F32)
        for i in range(NPIECE):
            s = dot_nt(keys_span[PIECE * i : PIECE * (i + 1), cols], rows) * SCALE
            if i == 0:
                s = jnp.where(hidden_first, LOW, s)
            if i == NPIECE - 1:
                s = jnp.where(hidden_last, LOW, s)
            exps[k, PIECE * i : PIECE * (i + 1), :] = s
            top = jnp.maximum(top, jnp.max(s.reshape(PIECE // 8, 8, 256), axis=0))
        top = jnp.max(top, axis=0, keepdims=True)
        summed = jnp.zeros((8, 256), F32)
        for i in range(NPIECE):
            e = jnp.exp(exps[k, PIECE * i : PIECE * (i + 1), :] - top)
            exps[k, PIECE * i : PIECE * (i + 1), :] = e
            if i == 0:
                e = e[EDGE:]
            if i == NPIECE - 1:
                e = e[: PIECE - EDGE]
            summed = summed + jnp.sum(e.reshape(-1, 8, 256), axis=0)
        summed = jnp.sum(summed, axis=0, keepdims=True)
        for n in range(2):
            here = stat_row == 2 * k + n
            tops = jnp.where(here, top[:, 128 * n : 128 * (n + 1)], tops)
            sums = jnp.where(here, summed[:, 128 * n : 128 * (n + 1)], sums)
        return tops, sums

    tops, sums = lax.fori_loop(
        0, KEY_HEADS, window_go, (jnp.zeros((CHIPS, 128), F32), jnp.zeros((CHIPS, 128), F32))
    )
    stat[0] = tops
    stat[1] = sums
    every(1, CHIPS, lambda d: stat_copy(lax.rem(p + d, CHIPS), p).start())
    stat_in[p] = stat[...]

    qt_self.wait()

    def qt_wait(r):
        @pl.when(r != slot)
        def _():
            remote(
                qt_in.at[r], qt_in.at[r], qt_send.at[0], qt_recv.at[r], core_of(8 * half + r), z
            ).wait_recv()

    every(0, 8, qt_wait)
    every(0, 4, lambda n: fwd_copy(n, 1 - j).wait_recv())
    rows_q = qt_in[:, 128:160, :].reshape(256, 128)

    def tail_go(r):
        s = dot_nt(qt_in[r, 128:160, :], qt_in[r, 0:128, :]) * SCALE
        tail_scores[r] = s + qt_in[r, 160:QT_ROWS, :].astype(F32)

    each(0, 8, tail_go)
    top = tail_scores[...].reshape(256, 128)

    def score_go(n, top):
        right = kv_in[pl.ds(4 * n, 4), 0:BLOCK, :].reshape(4 * BLOCK, 128)
        s = dot_nt(rows_q, right) * SCALE
        for i in range(4):
            bias = kv_in[4 * n + i, 2 * BLOCK : KV_ROWS, :].astype(F32)[0:1, :]
            one = s[:, BLOCK * i : BLOCK * (i + 1)] + bias
            dec_scores[n, :, BLOCK * i : BLOCK * (i + 1)] = one
            top = jnp.maximum(top, one)
        return top

    top = lax.fori_loop(0, CHIPS // 2, score_go, top)
    top = jnp.max(top, axis=1, keepdims=True)

    def split(weights):
        high = weights.astype(BF16)
        return high, (weights - high.astype(F32)).astype(BF16)

    tail_weights = jnp.exp(tail_scores[...].reshape(256, 128) - top)
    tail_acc = []
    for r in range(8):
        high, low = split(tail_weights[32 * r : 32 * (r + 1), :])
        right = qt_in[r, 64:QT_ROWS, :]
        tail_acc.append(dot(high, right) + dot(low, right))

    def value_go(n, carry):
        acc, weight_sum = carry
        weights = jnp.exp(dec_scores[n] - top)
        high, low = split(weights)
        right = kv_in[pl.ds(4 * n, 4), BLOCK : 2 * BLOCK, :].reshape(4 * BLOCK, 128)
        for i in range(4):
            weight_sum = weight_sum + weights[:, BLOCK * i : BLOCK * (i + 1)]
        return acc + (dot(high, right) + dot(low, right)), weight_sum

    acc, weight_sum = lax.fori_loop(
        0, CHIPS // 2, value_go, (jnp.concatenate(tail_acc, axis=0), tail_weights)
    )
    result = acc / jnp.sum(weight_sum, axis=1, keepdims=True)
    dec_send[...] = result.astype(BF16).reshape(8, 32, 128)

    def dec_copy(r):
        return remote(
            dec_send.at[r],
            dec_in.at[slot],
            dec_send_sem.at[r],
            dec_recv.at[slot],
            core_of(8 * half + r),
            z,
        )

    def dec_go(r):
        @pl.when(r != slot)
        def _():
            dec_copy(r).start()

    every(0, 8, dec_go)
    dec_self = pltpu.make_async_copy(dec_send.at[slot], dec_in.at[slot], local_sem.at[7])
    dec_self.start()

    every(
        1,
        CHIPS,
        lambda d: stat_copy(
            lax.rem(p + CHIPS - d, CHIPS), lax.rem(p + CHIPS - d, CHIPS)
        ).wait_recv(),
    )
    peak = stat_in[0, 0]
    for o in range(1, CHIPS):
        peak = jnp.maximum(peak, stat_in[o, 0])
    merged = jnp.zeros((CHIPS, 128), F32)
    for o in range(CHIPS):
        merged = merged + stat_in[o, 1] * jnp.exp(stat_in[o, 0] - peak)
    factor = jnp.exp(stat[0] - peak) / merged

    factors = [factor[o : o + 1, :] for o in range(CHIPS)]
    head_lane = lax.broadcasted_iota(jnp.int32, (PIECE, 128), 1)
    for i in range(NPIECE):
        rows = slice(PIECE * i, PIECE * (i + 1))
        votes = jnp.zeros((PIECE, 128), F32)
        for k in range(KEY_HEADS):
            weighted = (
                exps[k, rows, 0:128] * factors[2 * k] + exps[k, rows, 128:256] * factors[2 * k + 1]
            )
            votes = jnp.where(head_lane == k, jnp.sum(weighted, axis=1, keepdims=True), votes)
        columns[rows, :] = votes
    columns[ROWS:, :] = jnp.zeros((columns.shape[0] - ROWS, 128), F32)
    lanes = columns.shape[0]
    across = jnp.transpose(columns[...])[0:KEY_HEADS, :]
    near = POOL // 2
    window_sum = jnp.zeros((KEY_HEADS, lanes), F32)
    for shift in range(EDGE - near, EDGE + near + 1):
        window_sum = window_sum + pltpu.roll(across, lanes - shift, axis=1)
    for n in range(2):
        pooled[n] = window_sum[:, POSITIONS * n : POSITIONS * (n + 1)]
    share_votes = remote(pooled.at[1 - j], pooled_in, pair_send.at[4], pair_recv.at[4], sibling, z)
    share_votes.start()

    dec_self.wait()

    def dec_wait(k):
        @pl.when(k != slot)
        def _():
            remote(
                dec_send.at[k], dec_in.at[k], dec_send_sem.at[0], dec_recv.at[k], core_of(8 * half + k), z
            ).wait_recv()

    every(0, 8, dec_wait)
    rows_wide[...] = dec_in[...].astype(F32).reshape(256, 128)
    for h in range(64):
        decode_out[h] = rows_wide[4 * h : 4 * (h + 1), :].astype(BF16)

    share_votes.wait_recv()
    votes_out[...] = (pooled[j] + pooled_in[...]) * (
        2 * CHIPS * POSITIONS / (WIN * 8) / POOL
    )

    share_votes.wait_send()
    share_w.wait_send()
    share_k.wait_send()

    @pl.when(p < CHIPS - 1)
    def _():
        edge_copy(True).wait_send()

    @pl.when(p > 0)
    def _():
        edge_copy(False).wait_send()

    for d in range(1, PAIRS):
        q = lax.rem(pair + d, PAIRS)
        piece_copy(q, pair).wait_send()
        part_copy(0, q, pair, j).wait_send()
        part_copy(1, q, pair, j).wait_send()
    part_copy(1 - j, pair, pair, j).wait_send()
    for n in range(2):
        weight_copy(n).wait_send()
        weight_on(n).wait_send()

    def sent_chip(d):
        chip = lax.rem(p + d, CHIPS)
        gather_copy(chip, p).wait_send()
        window_copy(chip, p).wait_send()
        stat_copy(chip, p).wait_send()
        kv_copy(chip % 8, chip // 8).wait_send()

    each(1, CHIPS, sent_chip)
    each(0, 4, lambda n: fwd_copy(n, j).wait_send())

    def sent_slot(k):
        @pl.when(k != slot)
        def _():
            qt_copy(k).wait_send()
            dec_copy(k).wait_send()

    each(0, 8, sent_slot)


def on_device(
    window_states,
    query_weight,
    cache_keys,
    cache_values,
    kept_blocks,
    retained_block_count,
    decode_queries,
    tail_keys,
    tail_values,
    row_lengths,
):
    queries = decode_queries.reshape(STEPS, 64, HEAD_DIMENSION).transpose(1, 0, 2)
    hbm = pl.BlockSpec(memory_space=pl.ANY)
    vmem = pl.BlockSpec(memory_space=pltpu.VMEM)
    dma = pltpu.SemaphoreType.DMA
    votes, decoded = pl.pallas_call(
        body,
        out_shape=(
            jax.ShapeDtypeStruct((KEY_HEADS, POSITIONS), F32),
            jax.ShapeDtypeStruct((64, STEPS, HEAD_DIMENSION), BF16),
        ),
        in_specs=[hbm] * 11,
        out_specs=(vmem, vmem),
        scratch_shapes=[
            pltpu.VMEM((2, 2, 1024, 256), BF16),
            pltpu.VMEM((POSITIONS, 1024), BF16),
            pltpu.VMEM((POSITIONS, 1024), BF16),
            pltpu.VMEM((ROWS, 1024), BF16),
            pltpu.VMEM((CHIPS, PAIRS, 16, 256), BF16),
            pltpu.VMEM((2, PAIRS, 32, 256), F32),
            pltpu.VMEM((PAIRS, 2, 32, 256), F32),
            pltpu.VMEM((CHIPS, 2, WIN, 128), BF16),
            pltpu.VMEM((KEY_HEADS, ROWS, 256), F32),
            pltpu.VMEM((2, CHIPS, 128), F32),
            pltpu.VMEM((CHIPS, 2, CHIPS, 128), F32),
            pltpu.VMEM((ROWS + 96, 128), F32),
            pltpu.VMEM((2, KEY_HEADS, POSITIONS), F32),
            pltpu.VMEM((KEY_HEADS, POSITIONS), F32),
            pltpu.VMEM((KEY_HEADS, KV_ROWS, 128), BF16),
            pltpu.VMEM((2 * CHIPS, KV_ROWS, 128), BF16),
            pltpu.VMEM((KEY_HEADS, QT_ROWS, 128), BF16),
            pltpu.VMEM((8, QT_ROWS, 128), BF16),
            pltpu.VMEM((CHIPS // 2, 256, 4 * BLOCK), F32),
            pltpu.VMEM((8, 32, 128), F32),
            pltpu.VMEM((8, 32, 128), BF16),
            pltpu.VMEM((8, 32, 128), BF16),
            pltpu.VMEM((1, 8), jnp.int32),
            pltpu.VMEM((1, 8), jnp.int32),
            pltpu.VMEM((1, 1), jnp.int32),
            pltpu.VMEM((2, WIN, 128), F32),
            pltpu.VMEM((64, STEPS, 128), BF16),
            pltpu.VMEM((256, 128), F32),
            dma((40,)),
            dma((PAIRS,)),
            dma((PAIRS,)),
            dma((CHIPS,)),
            dma((CHIPS,)),
            dma((5,)),
            dma((5,)),
            dma((2, PAIRS)),
            dma((PAIRS, 2)),
            dma((CHIPS,)),
            dma((CHIPS,)),
            dma((CHIPS,)),
            dma((CHIPS,)),
            dma((4,)),
            dma((4,)),
            dma((CHIPS,)),
            dma((CHIPS,)),
            dma((4,)),
            dma((4,)),
            dma((8,)),
            dma((8,)),
            dma((8,)),
            dma((8,)),
        ],
        compiler_params=pltpu.CompilerParams(
            collective_id=0, has_side_effects=True, vmem_limit_bytes=60 * 1024 * 1024
        ),
        cost_estimate=pl.CostEstimate(
            flops=1_400_000_000, bytes_accessed=6_000_000, transcendentals=3_500_000
        ),
    )(
        window_states,
        query_weight,
        cache_keys,
        cache_values,
        kept_blocks.reshape(1, KEY_HEADS),
        retained_block_count.reshape(1, KEY_HEADS),
        queries,
        tail_keys,
        tail_values,
        row_lengths,
        jnp.asarray(rotary_table()),
    )
    decoded = decoded.transpose(1, 0, 2).reshape(1, STEPS, 1, 64 * HEAD_DIMENSION)
    return votes[None], decoded


def solution(mesh):
    placed = (
        P("grp", None, None),
        P("grp", "ctx"),
        P("grp", "ctx", None),
        P("grp", "ctx", None),
        P("grp", None, "ctx"),
        P("grp", None, "ctx"),
        P("grp", None, "ctx", None),
        P("grp", "ctx", None, None),
        P("grp", "ctx", None, None),
        P("grp", "ctx"),
    )
    return jax.shard_map(
        on_device,
        mesh=mesh,
        in_specs=placed,
        out_specs=(P("grp", None, "ctx"), P("grp", None, "ctx", None)),
        check_vma=False,
    )
```

```python
import math

import jax
import jax.numpy as jnp
import numpy as np
from jax import lax
from jax.experimental import pallas as pl
from jax.experimental.pallas import tpu as pltpu
from jax.sharding import PartitionSpec as P

MESH = pl.DeviceIdType.MESH
F32 = jnp.float32
BF16 = jnp.bfloat16
KEY_HEADS = 8
HEAD_DIMENSION = 128
BLOCK = 128
POOL = 7
WIN = 64
STEPS = 4
CHIPS = 16
GROUPS = 8
PAIRS = GROUPS // 2
POSITIONS = 512
SPAN = 2 * POSITIONS
EDGE = 16
ROWS = SPAN + 2 * EDGE
PIECE = 96
NPIECE = ROWS // PIECE
KV_ROWS = 2 * BLOCK + 16
QT_ROWS = 192
LOW = -1e30
SCALE = 1.0 / math.sqrt(HEAD_DIMENSION)
NT = (((1,), (1,)), ((), ()))


def rotary_table():
    exponent = np.arange(0, HEAD_DIMENSION, 2).astype(np.float32) / np.float32(HEAD_DIMENSION)
    inverse = np.power(np.float32(500000.0), -exponent).astype(np.float32)
    wavelength = np.float32(2.0 * math.pi) / inverse
    smooth = (np.float32(8192.0) / wavelength - np.float32(1.0)) / np.float32(3.0)
    blended = (np.float32(1.0) - smooth) * inverse / np.float32(8.0) + smooth * inverse
    adjusted = np.where(
        wavelength > 8192.0,
        inverse / np.float32(8.0),
        np.where(wavelength < 2048.0, inverse, blended),
    ).astype(np.float32)
    start = 2 * CHIPS * POSITIONS - WIN
    positions = (np.arange(WIN) + start).astype(np.float32)
    angles = (positions[:, None] * adjusted[None, :]).astype(np.float32).astype(np.float64)
    cosine, sine = np.cos(angles), np.sin(angles)
    return np.stack(
        [np.concatenate([cosine, cosine], axis=1), np.concatenate([-sine, sine], axis=1)]
    ).astype(np.float32)


def dot(a, b):
    return jnp.dot(a, b, preferred_element_type=F32)


def dot_nt(a, b):
    return lax.dot_general(a, b, NT, preferred_element_type=F32)


def body(
    states,
    weight,
    keys,
    values,
    kept,
    counts,
    queries,
    tail_keys,
    tail_values,
    lengths,
    turn,
    votes_out,
    decode_out,
    w_all,
    keys_own,
    values_own,
    keys_span,
    gathered,
    partial,
    parts,
    window,
    exps,
    stat,
    stat_in,
    columns,
    pooled,
    pooled_in,
    kv_out,
    kv_in,
    qt_out,
    qt_in,
    dec_scores,
    tail_scores,
    dec_send,
    dec_in,
    kept_own,
    counts_own,
    lengths_own,
    turn_own,
    queries_own,
    rows_wide,
    local_sem,
    piece_send,
    piece_recv,
    gather_send,
    gather_recv,
    pair_send,
    pair_recv,
    part_send,
    part_recv,
    window_send,
    window_recv,
    stat_send,
    stat_recv,
    weight_send,
    weight_recv,
    kv_send,
    kv_recv,
    fwd_send,
    fwd_recv,
    qt_send,
    qt_recv,
    dec_send_sem,
    dec_recv,
):
    c = lax.axis_index("ctx")
    z = lax.axis_index("grp")
    p = c // 2
    j = c % 2
    sibling = 2 * p + (1 - j)
    half = p // 8
    slot = p % 8

    def remote(src, dst, send_sem, recv_sem, ctx, grp):
        return pltpu.make_async_remote_copy(
            src_ref=src,
            dst_ref=dst,
            send_sem=send_sem,
            recv_sem=recv_sem,
            device_id=(ctx, grp),
            device_id_type=MESH,
        )

    def core_of(chip):
        return 2 * chip + j

    def each(low, high, step):
        def go(i, carry):
            step(i)
            return carry

        lax.fori_loop(low, high, go, 0)

    def every(low, high, step):
        for i in range(low, high):
            step(i)

    side = z % 2
    pair = z // 2
    other = 2 * pair + 1 - side

    barrier = pltpu.get_barrier_semaphore()

    def greet(ctx, grp):
        pl.semaphore_signal(barrier, inc=1, device_id=(ctx, grp), device_id_type=MESH)

    def group_of(d):
        return 2 * lax.rem(pair + d, PAIRS) + side

    for d in range(1, PAIRS):
        greet(c, group_of(d))
        greet(sibling, group_of(d))
    greet(c, other)
    greet(sibling, z)
    every(1, CHIPS, lambda d: greet(core_of(lax.rem(p + d, CHIPS)), z))

    own_rows = pl.ds(pl.multiple_of(EDGE + j * POSITIONS, 16), POSITIONS)
    load_w = pltpu.make_async_copy(weight, w_all.at[side, j], local_sem.at[0])
    load_k = pltpu.make_async_copy(keys.at[0], keys_own, local_sem.at[1])
    load_v = pltpu.make_async_copy(values.at[0], values_own, local_sem.at[2])
    load_span = pltpu.make_async_copy(keys.at[0], keys_span.at[own_rows], local_sem.at[3])
    row0 = pl.multiple_of(32 * j + 16 * (p // 8), 16)

    def piece_of(q):
        col0 = pl.multiple_of(q * 2048 + 256 * (p % 8), 256)
        return states.at[0, pl.ds(row0, 16), pl.ds(col0, 256)]

    load_piece = pltpu.make_async_copy(piece_of(pair), gathered.at[p, pair], local_sem.at[4])
    small = [
        pltpu.make_async_copy(src, dst, local_sem.at[32 + n])
        for n, (src, dst) in enumerate(
            (
                (kept, kept_own),
                (counts, counts_own),
                (lengths, lengths_own),
                (turn, turn_own),
                (queries, queries_own),
            )
        )
    ]

    def qt_load(k):
        cols = slice(k * 128, (k + 1) * 128)
        return (
            pltpu.make_async_copy(
                tail_keys.at[0, 0, :, cols], qt_out.at[k, 0:64], local_sem.at[8 + k]
            ),
            pltpu.make_async_copy(
                tail_values.at[0, 0, :, cols], qt_out.at[k, 64:128], local_sem.at[16 + k]
            ),
        )

    load_k.start()
    load_v.start()
    for copy in small:
        copy.start()
    load_piece.start()
    load_w.start()
    load_span.start()
    for k in range(KEY_HEADS):
        for copy in qt_load(k):
            copy.start()

    for copy in small:
        copy.wait()
    load_k.wait()
    load_v.wait()
    for k in range(KEY_HEADS):
        cols = slice(k * 128, (k + 1) * 128)
        block = jnp.broadcast_to(kept_own[:, k : k + 1], (BLOCK, 128)) - c * (POSITIONS // BLOCK)
        chosen = [
            jnp.where(block == b, 1.0, 0.0).astype(BF16) for b in range(POSITIONS // BLOCK)
        ]
        for n, own in ((0, keys_own), (1, values_own)):
            kv_out[k, n * BLOCK : (n + 1) * BLOCK, :] = sum(
                chosen[b] * own[b * BLOCK : (b + 1) * BLOCK, cols]
                for b in range(POSITIONS // BLOCK)
            )
        live = jnp.broadcast_to(counts_own[:, k : k + 1], (16, 128)) > 0
        kv_out[k, 2 * BLOCK : KV_ROWS, :] = jnp.where(live, 0.0, LOW).astype(BF16)
    step_row = lax.broadcasted_iota(jnp.int32, (32, 128), 0) % STEPS
    lane = lax.broadcasted_iota(jnp.int32, (32, 128), 1)
    tail_bias = jnp.where(
        lane < jnp.broadcast_to(lengths_own[...], (32, 128)) + step_row, 0.0, LOW
    ).astype(BF16)
    for k in range(KEY_HEADS):
        for h in range(8):
            rows_wide[32 * k + 4 * h : 32 * k + 4 * (h + 1), :] = queries_own[8 * k + h].astype(F32)
        qt_out[k, 128:160, :] = rows_wide[32 * k : 32 * (k + 1), :].astype(BF16)
        qt_out[k, 160:QT_ROWS, :] = tail_bias

    pl.semaphore_wait(barrier, CHIPS - 1 + 1 + 2 * (PAIRS - 1) + 1)

    def piece_copy(q_to, q_from):
        return remote(
            piece_of(q_to),
            gathered.at[p, q_from],
            piece_send.at[q_to],
            piece_recv.at[q_from],
            c,
            2 * q_to + side,
        )

    def pair_before(d):
        return lax.rem(pair + PAIRS - d, PAIRS)

    every(1, PAIRS, lambda d: piece_copy(lax.rem(pair + d, PAIRS), pair).start())

    def weight_copy(n):
        rows = pl.ds(512 * n, 512)
        return remote(
            weight.at[rows],
            w_all.at[side, j, rows],
            weight_send.at[n],
            weight_recv.at[n],
            c,
            other,
        )

    def weight_on(n):
        part = w_all.at[1 - side, j, pl.ds(512 * n, 512)]
        return remote(part, part, weight_send.at[2 + n], weight_recv.at[2 + n], sibling, z)

    share_w = remote(weight, w_all.at[side, j], pair_send.at[0], pair_recv.at[0], sibling, z)
    share_k = remote(keys.at[0], keys_span.at[own_rows], pair_send.at[1], pair_recv.at[1], sibling, z)
    weight_copy(0).start()
    weight_copy(1).start()
    share_w.start()

    load_piece.wait()
    every(1, PAIRS, lambda d: piece_copy(pair_before(d), pair_before(d)).wait_recv())

    def gather_copy(chip, source):
        return remote(
            gathered.at[source],
            gathered.at[source],
            gather_send.at[chip],
            gather_recv.at[source],
            core_of(chip),
            z,
        )

    every(1, CHIPS, lambda d: gather_copy(lax.rem(p + d, CHIPS), p).start())
    share_k.start()

    def kv_copy(k, half_to):
        chip = k + 8 * half_to
        return remote(
            kv_out.at[k],
            kv_in.at[j * CHIPS + p],
            kv_send.at[chip],
            kv_recv.at[p],
            core_of(chip),
            z,
        )

    def kv_go(d):
        chip = lax.rem(p + d, CHIPS)
        kv_copy(chip % 8, chip // 8).start()

    kv_self = pltpu.make_async_copy(kv_out.at[slot], kv_in.at[j * CHIPS + p], local_sem.at[5])
    kv_self.start()

    def qt_copy(k):
        return remote(
            qt_out.at[k],
            qt_in.at[slot],
            qt_send.at[k],
            qt_recv.at[slot],
            core_of(8 * half + k),
            z,
        )

    for k in range(KEY_HEADS):
        for copy in qt_load(k):
            copy.wait()

    qt_self = pltpu.make_async_copy(qt_out.at[slot], qt_in.at[slot], local_sem.at[6])
    qt_self.start()

    load_w.wait()
    share_w.wait_recv()
    every(
        1,
        CHIPS,
        lambda d: gather_copy(
            lax.rem(p + CHIPS - d, CHIPS), lax.rem(p + CHIPS - d, CHIPS)
        ).wait_recv(),
    )

    every(1, CHIPS, kv_go)

    def qt_go(k):
        @pl.when(k != slot)
        def _():
            qt_copy(k).start()

    every(0, KEY_HEADS, qt_go)

    def left_of(m):
        return jnp.concatenate(
            [gathered[m].reshape(64, 256), gathered[8 + m].reshape(64, 256)], axis=0
        )

    def product(core, group_side):
        acc = jnp.zeros((128, 256), F32)
        for m in range(4):
            acc = acc + dot(
                left_of(4 * group_side + m), w_all[group_side, core, 256 * m : 256 * (m + 1), :]
            )
        return acc

    for n in range(2):
        weight_copy(n).wait_recv()
        weight_on(n).start()
    for n in range(2):
        weight_on(n).wait_recv()
    for core in range(2):
        acc = (product(core, 0) + product(core, 1)).reshape(2, PAIRS, 16, 256)
        for i in range(2):
            partial[core, :, 16 * i : 16 * (i + 1), :] = acc[i]

    def part_copy(core, q_to, q_from, j_from):
        return remote(
            partial.at[core, q_to],
            parts.at[q_from, j_from],
            part_send.at[core, q_to],
            part_recv.at[q_from, j_from],
            2 * p + core,
            2 * q_to + side,
        )

    for d in range(1, PAIRS):
        q = lax.rem(pair + d, PAIRS)
        part_copy(0, q, pair, j).start()
        part_copy(1, q, pair, j).start()
    part_copy(1 - j, pair, pair, j).start()
    parts[pair, j] = partial[j, pair]

    load_span.wait()
    share_k.wait_recv()

    def edge_copy(up):
        src = keys_span.at[pl.ds(SPAN if up else EDGE, EDGE)]
        dst = keys_span.at[pl.ds(0 if up else SPAN + EDGE, EDGE)]
        chip = p + 1 if up else p - 1
        n = 2 + int(up)
        return remote(src, dst, pair_send.at[n], pair_recv.at[n], core_of(chip), z)

    @pl.when(p < CHIPS - 1)
    def _():
        edge_copy(True).start()

    @pl.when(p > 0)
    def _():
        edge_copy(False).start()

    @pl.when(p == 0)
    def _():
        keys_span[0:EDGE, :] = jnp.zeros((EDGE, 1024), BF16)

    @pl.when(p == CHIPS - 1)
    def _():
        keys_span[SPAN + EDGE : ROWS, :] = jnp.zeros((EDGE, 1024), BF16)

    for d in range(1, PAIRS):
        part_copy(0, pair_before(d), pair_before(d), 0).wait_recv()
        part_copy(0, pair_before(d), pair_before(d), 1).wait_recv()
    part_copy(0, pair, pair, 1 - j).wait_recv()
    for i in range(2):
        summed = parts[0, i]
        for q in range(1, PAIRS):
            summed = summed + parts[q, i]
        turn_c = turn_own[0, 32 * i : 32 * (i + 1), :]
        turn_s = turn_own[1, 32 * i : 32 * (i + 1), :]
        for h in range(2):
            head = summed[:, 128 * h : 128 * (h + 1)]
            turned = head * turn_c + pltpu.roll(head, 64, axis=1) * turn_s
            window[p, h, 32 * i : 32 * (i + 1), :] = turned.astype(BF16)

    def window_copy(chip, source):
        return remote(
            window.at[source],
            window.at[source],
            window_send.at[chip],
            window_recv.at[source],
            core_of(chip),
            z,
        )

    every(1, CHIPS, lambda d: window_copy(lax.rem(p + d, CHIPS), p).start())

    kv_self.wait()

    def kv_wait(source):
        @pl.when(source != p)
        def _():
            remote(
                kv_in.at[j * CHIPS + source],
                kv_in.at[j * CHIPS + source],
                kv_send.at[0],
                kv_recv.at[source],
                core_of(source),
                z,
            ).wait_recv()

    def fwd_copy(n, core):
        part = kv_in.at[pl.ds(core * CHIPS + 4 * n, 4)]
        return remote(part, part, fwd_send.at[n], fwd_recv.at[n], sibling, z)

    for n in range(4):
        every(4 * n, 4 * n + 4, kv_wait)
        fwd_copy(n, j).start()


    qt_self.wait()

    def qt_wait(r):
        @pl.when(r != slot)
        def _():
            remote(
                qt_in.at[r], qt_in.at[r], qt_send.at[0], qt_recv.at[r], core_of(8 * half + r), z
            ).wait_recv()

    every(0, 8, qt_wait)
    rows_q = qt_in[:, 128:160, :].reshape(256, 128)

    def tail_go(r):
        s = dot_nt(qt_in[r, 128:160, :], qt_in[r, 0:128, :]) * SCALE
        tail_scores[r] = s + qt_in[r, 160:QT_ROWS, :].astype(F32)

    each(0, 8, tail_go)
    top = tail_scores[...].reshape(256, 128)

    def score_go(n, top):
        right = kv_in[pl.ds(4 * n, 4), 0:BLOCK, :].reshape(4 * BLOCK, 128)
        s = dot_nt(rows_q, right) * SCALE
        for i in range(4):
            bias = kv_in[4 * n + i, 2 * BLOCK : KV_ROWS, :].astype(F32)[0:1, :]
            one = s[:, BLOCK * i : BLOCK * (i + 1)] + bias
            dec_scores[n, :, BLOCK * i : BLOCK * (i + 1)] = one
            top = jnp.maximum(top, one)
        return top

    top_near = lax.fori_loop(0, 4, lambda n, t: score_go(4 * j + n, t), top)

    @pl.when(p > 0)
    def _():
        edge_copy(True).wait_recv()

    @pl.when(p < CHIPS - 1)
    def _():
        edge_copy(False).wait_recv()

    piece_row = lax.broadcasted_iota(jnp.int32, (PIECE, 256), 0)
    piece_lane = lax.broadcasted_iota(jnp.int32, (PIECE, 256), 1)
    hidden_first = jnp.logical_and(piece_row < EDGE, p == 0)
    last_row = piece_row + (NPIECE - 1) * PIECE
    hidden_last = jnp.logical_or(
        jnp.logical_and(last_row >= SPAN + EDGE, p == CHIPS - 1),
        jnp.logical_and(
            last_row < SPAN + EDGE,
            p * SPAN + last_row - EDGE
            > (2 * CHIPS * POSITIONS - WIN) + jnp.bitwise_and(piece_lane, WIN - 1),
        ),
    )

    def stat_copy(chip, source):
        return remote(
            stat, stat_in.at[source], stat_send.at[chip], stat_recv.at[source], core_of(chip), z
        )

    stat_row = lax.broadcasted_iota(jnp.int32, (CHIPS, 128), 0)

    def window_go(k, carry):
        tops, sums = carry
        for n in range(2):
            source = 2 * k + n

            @pl.when(source != p)
            def _():
                window_copy(0, source).wait_recv()

        rows = window[pl.ds(2 * k, 2)].reshape(256, 128)
        cols = pl.ds(pl.multiple_of(k * 128, 128), 128)
        top = jnp.full((8, 256), LOW, F32)
        for i in range(NPIECE):
            s = dot_nt(keys_span[PIECE * i : PIECE * (i + 1), cols], rows) * SCALE
            if i == 0:
                s = jnp.where(hidden_first, LOW, s)
            if i == NPIECE - 1:
                s = jnp.where(hidden_last, LOW, s)
            exps[k, PIECE * i : PIECE * (i + 1), :] = s
            top = jnp.maximum(top, jnp.max(s.reshape(PIECE // 8, 8, 256), axis=0))
        top = jnp.max(top, axis=0, keepdims=True)
        summed = jnp.zeros((8, 256), F32)
        for i in range(NPIECE):
            e = jnp.exp(exps[k, PIECE * i : PIECE * (i + 1), :] - top)
            exps[k, PIECE * i : PIECE * (i + 1), :] = e
            if i == 0:
                e = e[EDGE:]
            if i == NPIECE - 1:
                e = e[: PIECE - EDGE]
            summed = summed + jnp.sum(e.reshape(-1, 8, 256), axis=0)
        summed = jnp.sum(summed, axis=0, keepdims=True)
        for n in range(2):
            here = stat_row == 2 * k + n
            tops = jnp.where(here, top[:, 128 * n : 128 * (n + 1)], tops)
            sums = jnp.where(here, summed[:, 128 * n : 128 * (n + 1)], sums)
        return tops, sums

    tops, sums = lax.fori_loop(
        0, KEY_HEADS, window_go, (jnp.zeros((CHIPS, 128), F32), jnp.zeros((CHIPS, 128), F32))
    )
    stat[0] = tops
    stat[1] = sums
    every(1, CHIPS, lambda d: stat_copy(lax.rem(p + d, CHIPS), p).start())
    stat_in[p] = stat[...]

    every(0, 4, lambda n: fwd_copy(n, 1 - j).wait_recv())
    top = lax.fori_loop(0, 4, lambda n, t: score_go(4 * (1 - j) + n, t), top_near)
    top = jnp.max(top, axis=1, keepdims=True)

    def split(weights):
        high = weights.astype(BF16)
        return high, (weights - high.astype(F32)).astype(BF16)

    tail_weights = jnp.exp(tail_scores[...].reshape(256, 128) - top)
    tail_acc = []
    for r in range(8):
        high, low = split(tail_weights[32 * r : 32 * (r + 1), :])
        right = qt_in[r, 64:QT_ROWS, :]
        tail_acc.append(dot(high, right) + dot(low, right))

    def value_go(n, carry):
        acc, weight_sum = carry
        weights = jnp.exp(dec_scores[n] - top)
        high, low = split(weights)
        right = kv_in[pl.ds(4 * n, 4), BLOCK : 2 * BLOCK, :].reshape(4 * BLOCK, 128)
        for i in range(4):
            weight_sum = weight_sum + weights[:, BLOCK * i : BLOCK * (i + 1)]
        return acc + (dot(high, right) + dot(low, right)), weight_sum

    acc, weight_sum = lax.fori_loop(
        0, CHIPS // 2, value_go, (jnp.concatenate(tail_acc, axis=0), tail_weights)
    )
    result = acc / jnp.sum(weight_sum, axis=1, keepdims=True)
    dec_send[...] = result.astype(BF16).reshape(8, 32, 128)

    def dec_copy(r):
        return remote(
            dec_send.at[r],
            dec_in.at[slot],
            dec_send_sem.at[r],
            dec_recv.at[slot],
            core_of(8 * half + r),
            z,
        )

    def dec_go(r):
        @pl.when(r != slot)
        def _():
            dec_copy(r).start()

    every(0, 8, dec_go)
    dec_self = pltpu.make_async_copy(dec_send.at[slot], dec_in.at[slot], local_sem.at[7])
    dec_self.start()

    every(
        1,
        CHIPS,
        lambda d: stat_copy(
            lax.rem(p + CHIPS - d, CHIPS), lax.rem(p + CHIPS - d, CHIPS)
        ).wait_recv(),
    )
    peak = stat_in[0, 0]
    for o in range(1, CHIPS):
        peak = jnp.maximum(peak, stat_in[o, 0])
    merged = jnp.zeros((CHIPS, 128), F32)
    for o in range(CHIPS):
        merged = merged + stat_in[o, 1] * jnp.exp(stat_in[o, 0] - peak)
    factor = jnp.exp(stat[0] - peak) / merged

    factors = [factor[o : o + 1, :] for o in range(CHIPS)]
    head_lane = lax.broadcasted_iota(jnp.int32, (PIECE, 128), 1)
    for i in range(NPIECE):
        rows = slice(PIECE * i, PIECE * (i + 1))
        votes = jnp.zeros((PIECE, 128), F32)
        for k in range(KEY_HEADS):
            weighted = (
                exps[k, rows, 0:128] * factors[2 * k] + exps[k, rows, 128:256] * factors[2 * k + 1]
            )
            votes = jnp.where(head_lane == k, jnp.sum(weighted, axis=1, keepdims=True), votes)
        columns[rows, :] = votes
    columns[ROWS:, :] = jnp.zeros((columns.shape[0] - ROWS, 128), F32)
    lanes = columns.shape[0]
    across = jnp.transpose(columns[...])[0:KEY_HEADS, :]
    near = POOL // 2
    window_sum = jnp.zeros((KEY_HEADS, lanes), F32)
    for shift in range(EDGE - near, EDGE + near + 1):
        window_sum = window_sum + pltpu.roll(across, lanes - shift, axis=1)
    for n in range(2):
        pooled[n] = window_sum[:, POSITIONS * n : POSITIONS * (n + 1)]
    share_votes = remote(pooled.at[1 - j], pooled_in, pair_send.at[4], pair_recv.at[4], sibling, z)
    share_votes.start()

    dec_self.wait()

    def dec_wait(k):
        @pl.when(k != slot)
        def _():
            remote(
                dec_send.at[k], dec_in.at[k], dec_send_sem.at[0], dec_recv.at[k], core_of(8 * half + k), z
            ).wait_recv()

    every(0, 8, dec_wait)
    rows_wide[...] = dec_in[...].astype(F32).reshape(256, 128)
    for h in range(64):
        decode_out[h] = rows_wide[4 * h : 4 * (h + 1), :].astype(BF16)

    share_votes.wait_recv()
    votes_out[...] = (pooled[j] + pooled_in[...]) * (
        2 * CHIPS * POSITIONS / (WIN * 8) / POOL
    )

    share_votes.wait_send()
    share_w.wait_send()
    share_k.wait_send()

    @pl.when(p < CHIPS - 1)
    def _():
        edge_copy(True).wait_send()

    @pl.when(p > 0)
    def _():
        edge_copy(False).wait_send()

    for d in range(1, PAIRS):
        q = lax.rem(pair + d, PAIRS)
        piece_copy(q, pair).wait_send()
        part_copy(0, q, pair, j).wait_send()
        part_copy(1, q, pair, j).wait_send()
    part_copy(1 - j, pair, pair, j).wait_send()
    for n in range(2):
        weight_copy(n).wait_send()
        weight_on(n).wait_send()

    def sent_chip(d):
        chip = lax.rem(p + d, CHIPS)
        gather_copy(chip, p).wait_send()
        window_copy(chip, p).wait_send()
        stat_copy(chip, p).wait_send()
        kv_copy(chip % 8, chip // 8).wait_send()

    each(1, CHIPS, sent_chip)
    each(0, 4, lambda n: fwd_copy(n, j).wait_send())

    def sent_slot(k):
        @pl.when(k != slot)
        def _():
            qt_copy(k).wait_send()
            dec_copy(k).wait_send()

    each(0, 8, sent_slot)


def on_device(
    window_states,
    query_weight,
    cache_keys,
    cache_values,
    kept_blocks,
    retained_block_count,
    decode_queries,
    tail_keys,
    tail_values,
    row_lengths,
):
    queries = decode_queries.reshape(STEPS, 64, HEAD_DIMENSION).transpose(1, 0, 2)
    hbm = pl.BlockSpec(memory_space=pl.ANY)
    vmem = pl.BlockSpec(memory_space=pltpu.VMEM)
    dma = pltpu.SemaphoreType.DMA
    votes, decoded = pl.pallas_call(
        body,
        out_shape=(
            jax.ShapeDtypeStruct((KEY_HEADS, POSITIONS), F32),
            jax.ShapeDtypeStruct((64, STEPS, HEAD_DIMENSION), BF16),
        ),
        in_specs=[hbm] * 11,
        out_specs=(vmem, vmem),
        scratch_shapes=[
            pltpu.VMEM((2, 2, 1024, 256), BF16),
            pltpu.VMEM((POSITIONS, 1024), BF16),
            pltpu.VMEM((POSITIONS, 1024), BF16),
            pltpu.VMEM((ROWS, 1024), BF16),
            pltpu.VMEM((CHIPS, PAIRS, 16, 256), BF16),
            pltpu.VMEM((2, PAIRS, 32, 256), F32),
            pltpu.VMEM((PAIRS, 2, 32, 256), F32),
            pltpu.VMEM((CHIPS, 2, WIN, 128), BF16),
            pltpu.VMEM((KEY_HEADS, ROWS, 256), F32),
            pltpu.VMEM((2, CHIPS, 128), F32),
            pltpu.VMEM((CHIPS, 2, CHIPS, 128), F32),
            pltpu.VMEM((ROWS + 96, 128), F32),
            pltpu.VMEM((2, KEY_HEADS, POSITIONS), F32),
            pltpu.VMEM((KEY_HEADS, POSITIONS), F32),
            pltpu.VMEM((KEY_HEADS, KV_ROWS, 128), BF16),
            pltpu.VMEM((2 * CHIPS, KV_ROWS, 128), BF16),
            pltpu.VMEM((KEY_HEADS, QT_ROWS, 128), BF16),
            pltpu.VMEM((8, QT_ROWS, 128), BF16),
            pltpu.VMEM((CHIPS // 2, 256, 4 * BLOCK), F32),
            pltpu.VMEM((8, 32, 128), F32),
            pltpu.VMEM((8, 32, 128), BF16),
            pltpu.VMEM((8, 32, 128), BF16),
            pltpu.VMEM((1, 8), jnp.int32),
            pltpu.VMEM((1, 8), jnp.int32),
            pltpu.VMEM((1, 1), jnp.int32),
            pltpu.VMEM((2, WIN, 128), F32),
            pltpu.VMEM((64, STEPS, 128), BF16),
            pltpu.VMEM((256, 128), F32),
            dma((40,)),
            dma((PAIRS,)),
            dma((PAIRS,)),
            dma((CHIPS,)),
            dma((CHIPS,)),
            dma((5,)),
            dma((5,)),
            dma((2, PAIRS)),
            dma((PAIRS, 2)),
            dma((CHIPS,)),
            dma((CHIPS,)),
            dma((CHIPS,)),
            dma((CHIPS,)),
            dma((4,)),
            dma((4,)),
            dma((CHIPS,)),
            dma((CHIPS,)),
            dma((4,)),
            dma((4,)),
            dma((8,)),
            dma((8,)),
            dma((8,)),
            dma((8,)),
        ],
        compiler_params=pltpu.CompilerParams(
            collective_id=0, has_side_effects=True, vmem_limit_bytes=60 * 1024 * 1024
        ),
        cost_estimate=pl.CostEstimate(
            flops=1_400_000_000, bytes_accessed=6_000_000, transcendentals=3_500_000
        ),
    )(
        window_states,
        query_weight,
        cache_keys,
        cache_values,
        kept_blocks.reshape(1, KEY_HEADS),
        retained_block_count.reshape(1, KEY_HEADS),
        queries,
        tail_keys,
        tail_values,
        row_lengths,
        jnp.asarray(rotary_table()),
    )
    decoded = decoded.transpose(1, 0, 2).reshape(1, STEPS, 1, 64 * HEAD_DIMENSION)
    return votes[None], decoded


def solution(mesh):
    placed = (
        P("grp", None, None),
        P("grp", "ctx"),
        P("grp", "ctx", None),
        P("grp", "ctx", None),
        P("grp", None, "ctx"),
        P("grp", None, "ctx"),
        P("grp", None, "ctx", None),
        P("grp", "ctx", None, None),
        P("grp", "ctx", None, None),
        P("grp", "ctx"),
    )
    return jax.shard_map(
        on_device,
        mesh=mesh,
        in_specs=placed,
        out_specs=(P("grp", None, "ctx"), P("grp", None, "ctx", None)),
        check_vma=False,
    )
```
